32 devices in a mesh: region: 8 (over z, x), obs: 4 (over y, core).
Axes of the slice: x: 2, y: 2, z: 4, core: 2. Of those that a mesh axis runs over, the one named last changes fastest.
Arguments:
- pattern: int32 [262144], P(('region', 'obs')), may hold values from 0 to 511
- amplitude: float32 [5, 262144], P(None, ('region', 'obs')), may hold values from 0.5 to 1.5
- basis_table: bfloat16 [5, 512, 128], replicated, may hold values from -2 to 2, as said below
- fields: bfloat16 [64, 262144], P(None, ('region', 'obs')), may hold values from -24 to 24
- prior_precision: float32 [5, 128], replicated, may hold values from 16 to 512
Outputs:
- fitted: float32 [64, 262144], P(None, ('region', 'obs'))
The draws below stay inside these ranges and needn't reach their ends.
Inputs may be any that keep to these rules, and one draw needn't show every extreme that they name: `basis_table`: basis rows of different tiers for one pattern are correlated.
All inputs are finite; a program needn't handle non-finite values.
Results may differ from the reference program's by a relative error of at most 0.0062.
Values sent between devices are 32-bit elements; how exact they have to be, the bound alone decides.
No kernel may reach another device: no remote copies, remote signals or barrier semaphores. Data moves between devices by JAX's collectives and lax.ppermute only.
A program may use at most 64 MiB of HBM per device.

```python
import math
from functools import partial
import jax
import jax.numpy as jnp
from jax import lax

KNOTS = 128
FIELDS = 64
PATTERNS = 512
ANCESTORS = 4
TIERS = 5
LEAF_OBS = 32768
OBSERVATIONS = 262144
N_REGION = 8


def draw_basis_table(key, part):
    shared_key, own_key = jax.random.split(jax.random.fold_in(key, 7))
    shared = jnp.clip(jax.random.normal(shared_key, (PATTERNS, KNOTS), jnp.float32), -4.0, 4.0)
    own = jnp.clip(jax.random.normal(own_key, (TIERS, PATTERNS, KNOTS), jnp.float32), -4.0, 4.0)
    mixed = (0.6 * shared[None] + 0.8 * own) * KNOTS ** (-0.5)
    return mixed.astype(jnp.bfloat16)


def touch_ends(result, stream_key, smallest, top_value):
    spot = [jax.random.randint(jax.random.fold_in(stream_key, axis), (), 0, length) for axis, length in enumerate(result.shape)]
    main_axis = result.shape.index(max(result.shape))
    beside = spot[:main_axis] + [(spot[main_axis] + 1) % result.shape[main_axis]] + spot[main_axis + 1:]
    return result.at[tuple(spot)].set(smallest).at[tuple(beside)].set(top_value)


def block_scale(rng, extent, cuts, smallest, largest):
    factor_of = 1.0
    for position, blocks in cuts:
        heights = jax.random.uniform(jax.random.fold_in(jax.random.fold_in(rng, 6), position), (blocks,), jnp.float32, smallest / len(cuts), largest / len(cuts))
        factor_of = factor_of * jnp.repeat(jnp.exp(heights), extent[position] // blocks).reshape((-1,) + (1,) * (len(extent) - 1 - position))
    return factor_of


def bell_draw(stream_key, dims, scale, most, cuts=(), dtype=jnp.bfloat16):
    factor_of = block_scale(stream_key, dims, cuts, -0.22, 0.18) if cuts else 1.0
    values = jax.random.normal(stream_key, dims, jnp.float32) * scale * factor_of
    return jnp.minimum(jnp.maximum(values, -most), most).astype(dtype)


def setup_inputs(seed: int = 0) -> dict:
    streams_of = jax.random.split(jax.random.key(seed), 6)
    return {
        "pattern": touch_ends(jax.random.randint(streams_of[0], (OBSERVATIONS,), 0, PATTERNS), jax.random.fold_in(streams_of[0], 1), 0, PATTERNS - 1).astype(jnp.int32),
        "amplitude": jnp.clip(0.5 + 1.0 * jax.random.uniform(streams_of[1], (TIERS, OBSERVATIONS), jnp.float32) ** block_scale(streams_of[1], (TIERS, OBSERVATIONS), ((1, 32),), -0.2, 0.2), 0.5, 1.5),
        "basis_table": draw_basis_table(jax.random.fold_in(streams_of[5], 71), 0),
        "fields": bell_draw(streams_of[3], (FIELDS, OBSERVATIONS), 4.0, 24.0, ((1, 32),)),
        "prior_precision": jnp.clip(jnp.exp(jax.random.uniform(streams_of[4], (TIERS, KNOTS), jnp.float32, math.log(16.0), math.log(512.0))), 16.0, 512.0),
    }


highest = lax.Precision.HIGHEST

def basis_rows(basis_table, pattern_rows, amplitude_rows):
    blocks = []
    for tier_index in range(basis_table.shape[0]):
        picked = jnp.take(basis_table[tier_index], pattern_rows, axis=0).astype(jnp.float32)
        blocks.append((picked * amplitude_rows[tier_index][:, None]).astype(jnp.bfloat16))
    return jnp.concatenate(blocks, axis=1)

def add_prior(matrix, prior_precision, tier_index):
    offset = tier_index * prior_precision.shape[1]
    return matrix.at[offset:, offset:].add(jnp.diag(prior_precision[tier_index]))

def eliminate(matrix, rhs_rows, tier_index, knot_count):
    offset = tier_index * knot_count
    factor = jnp.linalg.cholesky(matrix[offset:, offset:])
    whiten = lax.linalg.triangular_solve(factor, rhs_rows[:, offset:].T, left_side=True, lower=True)
    coupling = lax.linalg.triangular_solve(factor, matrix[offset:, :offset], left_side=True, lower=True)
    schur_part = matrix[:offset, :offset] - jnp.dot(coupling.T, coupling, precision=highest)
    reduced = rhs_rows[:, :offset] - jnp.dot(whiten.T, coupling, precision=highest)
    return (factor, coupling, whiten, schur_part, reduced)

def descend(factor, coupling, whiten, path):
    target = whiten - jnp.dot(coupling, path, precision=highest)
    return lax.linalg.triangular_solve(factor, target, left_side=True, lower=True, transpose_a=True)

def reference(pattern, amplitude, basis_table, fields, prior_precision):
    leaves = N_REGION
    pattern_leaf = pattern.reshape(leaves, LEAF_OBS)
    amplitude_leaf = amplitude.reshape(TIERS, leaves, LEAF_OBS).transpose(1, 0, 2)
    fields_leaf = fields.reshape(FIELDS, leaves, LEAF_OBS).transpose(1, 0, 2)

    def leaf_moments(inputs):
        pattern_rows, amplitude_rows, field_rows = inputs
        design = basis_rows(basis_table, pattern_rows, amplitude_rows)
        cross = lax.dot_general(design.astype(jnp.float32), design.astype(jnp.float32), (((0,), (0,)), ((), ())), preferred_element_type=jnp.float32)
        project = jnp.dot(field_rows.astype(jnp.float32), design.astype(jnp.float32), preferred_element_type=jnp.float32)
        return (cross, project)
    matrix, rhs_rows = lax.map(leaf_moments, (pattern_leaf, amplitude_leaf, fields_leaf))
    matrix = jax.vmap(partial(add_prior, prior_precision=prior_precision, tier_index=ANCESTORS))(matrix)
    stored = {}
    for tier_index in range(ANCESTORS, 0, -1):
        step_fn = partial(eliminate, tier_index=tier_index, knot_count=KNOTS)
        factor, coupling, whiten, schur_part, reduced = jax.vmap(step_fn)(matrix, rhs_rows)
        stored[tier_index] = (factor, coupling, whiten)
        if tier_index > 1:
            schur_part = schur_part.reshape((schur_part.shape[0] // 2, 2) + schur_part.shape[1:]).sum(axis=1)
            reduced = reduced.reshape((reduced.shape[0] // 2, 2) + reduced.shape[1:]).sum(axis=1)
        else:
            schur_part = schur_part.sum(axis=0, keepdims=True)
            reduced = reduced.sum(axis=0, keepdims=True)
        matrix = jax.vmap(partial(add_prior, prior_precision=prior_precision, tier_index=tier_index - 1))(schur_part)
        rhs_rows = reduced
    root_factor = jnp.linalg.cholesky(matrix[0])
    root_whiten = lax.linalg.triangular_solve(root_factor, rhs_rows[0].T, left_side=True, lower=True)
    root_weight = lax.linalg.triangular_solve(root_factor, root_whiten, left_side=True, lower=True, transpose_a=True)
    path = root_weight[None]
    for tier_index in range(1, TIERS):
        factor, coupling, whiten = stored[tier_index]
        parent_path = jnp.repeat(path, factor.shape[0] // path.shape[0], axis=0)
        local = jax.vmap(descend)(factor, coupling, whiten, parent_path)
        path = jnp.concatenate([parent_path, local], axis=1)
    path_weights = path.astype(jnp.bfloat16)

    def leaf_fitted(inputs):
        pattern_rows, amplitude_rows, weights = inputs
        design = basis_rows(basis_table, pattern_rows, amplitude_rows)
        return lax.dot_general(weights.astype(jnp.float32), design.astype(jnp.float32), (((0,), (1,)), ((), ())), preferred_element_type=jnp.float32)
    fitted_leaf = lax.map(leaf_fitted, (pattern_leaf, amplitude_leaf, path_weights))
    return fitted_leaf.transpose(1, 0, 2).reshape(FIELDS, leaves * LEAF_OBS)
```

```python
import functools

import jax
import jax.numpy as jnp
from jax import lax
from jax.experimental import pallas as pl
from jax.experimental.pallas import tpu as pltpu
from jax.sharding import PartitionSpec as P

highest = lax.Precision.HIGHEST
f32 = jnp.float32
bf16 = jnp.bfloat16
SUB = 8
vmem = pl.BlockSpec(memory_space=pltpu.VMEM)


def pair_index(tier, other):
    return tier * (tier + 1) // 2 + other


def dot(a, b):
    return jnp.dot(a, b, preferred_element_type=f32)


def dot_nt(a, b, precision=None):
    return lax.dot_general(
        a, b, (((1,), (1,)), ((), ())), precision=precision, preferred_element_type=f32
    )


def dot_tn(a, b):
    return lax.dot_general(
        a, b, (((0,), (0,)), ((), ())), precision=highest, preferred_element_type=f32
    )


def dot_hi(a, b):
    return jnp.dot(a, b, precision=highest, preferred_element_type=f32)


def split(value):
    high = value.astype(bf16)
    return high, (value - high.astype(f32)).astype(bf16)


def one_hot(pattern_row, pattern_count):
    rows = lax.broadcasted_iota(jnp.int32, (pattern_count, pattern_row.shape[1]), 0)
    return jnp.where(rows == pattern_row, 1.0, 0.0).astype(bf16)


def stats_kernel(pattern_ref, amplitude_ref, fields_ref, basis_ref, pairs_ref, project_ref,
                 prods, acc):
    step = pl.program_id(0)
    tier_count, pattern_count, knots = basis_ref.shape
    field_count = fields_ref.shape[0]
    pair_rows = prods.shape[0]
    amp = amplitude_ref[...]
    prods[...] = jnp.zeros_like(prods)
    for tier in range(tier_count):
        first = pair_index(tier, 0)
        prods[first:first + tier + 1, :] = amp[:tier + 1] * amp[tier:tier + 1]
    pair_high, pair_low = split(prods[...])
    field_rows = fields_ref[...].astype(f32)
    weighted = [split(field_rows * amp[tier:tier + 1]) for tier in range(tier_count)]
    values = jnp.concatenate(
        [pair_high, pair_low] + [w[0] for w in weighted] + [w[1] for w in weighted], axis=0
    )
    part = dot_nt(values, one_hot(pattern_ref[...], pattern_count))

    @pl.when(step == 0)
    def _():
        acc[...] = part

    @pl.when(step > 0)
    def _():
        acc[...] += part

    @pl.when(step == pl.num_programs(0) - 1)
    def _():
        pairs_ref[...] = acc[:pair_rows] + acc[pair_rows:2 * pair_rows]
        base = 2 * pair_rows
        low_base = base + tier_count * field_count
        for tier in range(tier_count):
            first = base + tier * field_count
            second = low_base + tier * field_count
            high, low = split(acc[first:first + field_count] + acc[second:second + field_count])
            project_ref[:, tier * knots:(tier + 1) * knots] = (
                dot(high, basis_ref[tier]) + dot(low, basis_ref[tier])
            )


def statistics(pattern, amplitude, fields, basis_table):
    tier_count, pattern_count, knots = basis_table.shape
    field_count, obs = fields.shape
    block = min(2048, obs)
    pair_rows = -(-pair_index(tier_count, 0) // 16) * 16
    rows = 2 * pair_rows + 2 * tier_count * field_count
    return pl.pallas_call(
        stats_kernel,
        grid=(obs // block,),
        in_specs=[
            pl.BlockSpec((1, block), lambda i: (0, i)),
            pl.BlockSpec((tier_count, block), lambda i: (0, i)),
            pl.BlockSpec((field_count, block), lambda i: (0, i)),
            pl.BlockSpec(basis_table.shape, lambda i: (0, 0, 0)),
        ],
        out_specs=[
            pl.BlockSpec((pair_rows, pattern_count), lambda i: (0, 0)),
            pl.BlockSpec((field_count, tier_count * knots), lambda i: (0, 0)),
        ],
        out_shape=[
            jax.ShapeDtypeStruct((pair_rows, pattern_count), f32),
            jax.ShapeDtypeStruct((field_count, tier_count * knots), f32),
        ],
        scratch_shapes=[
            pltpu.VMEM((pair_rows, block), f32),
            pltpu.VMEM((rows, pattern_count), f32),
        ],
        compiler_params=pltpu.CompilerParams(vmem_limit_bytes=48 * 2**20),
        cost_estimate=pl.CostEstimate(
            flops=2 * rows * pattern_count * obs, bytes_accessed=4 * 2**20, transcendentals=0
        ),
        name="statistics",
    )(pattern.reshape(1, obs), amplitude, fields, basis_table)


def along_rows(x, row):
    return jnp.broadcast_to(x[row:row + 1, :], x.shape)


def along_lanes(x, lane):
    return jnp.broadcast_to(x[:, lane:lane + 1], x.shape)


def reciprocal(x):
    first = pltpu.reciprocal(x, approx=True)
    first = first * (2.0 - x * first)
    return first * (2.0 - x * first)


def solve_block(d, rows):
    count = len(d)
    factor = [[[None] * SUB for _ in range(SUB)] for _ in range(count)]
    inverse = [[None] * SUB for _ in range(count)]
    for k in range(SUB):
        for m in range(count):
            inverse[m][k] = reciprocal(d[m][k][k])
        for j in range(k + 1, SUB):
            for m in range(count):
                factor[m][j][k] = d[m][j][k] * inverse[m][k]
        for j in range(k + 1, SUB):
            for m in range(count):
                for i in range(j, SUB):
                    d[m][i][j] = d[m][i][j] - d[m][i][k] * factor[m][j][k]
                rows[m][j] = rows[m][j] - factor[m][j][k] * rows[m][k]
    for k in range(SUB):
        for m in range(count):
            rows[m][k] = rows[m][k] * inverse[m][k]
    for k in range(SUB - 1, -1, -1):
        for i in range(k):
            for m in range(count):
                rows[m][i] = rows[m][i] - factor[m][k][i] * rows[m][k]
    return rows


def sweep(rows, pivot, lane0, sub, lane):
    count, blocks = len(rows), len(rows[0])
    here = (lane >= lane0) & (lane < lane0 + SUB)
    eye = (lane - lane0 == sub).astype(f32)
    columns = [[along_lanes(rows[m][pivot], lane0 + j) for j in range(SUB)] for m in range(count)]
    d = [
        [[along_rows(columns[m][j], i) if j <= i else None for j in range(SUB)] for i in range(SUB)]
        for m in range(count)
    ]
    solved = []
    for m in range(count):
        start = jnp.where(here, eye, rows[m][pivot])
        solved.append([along_rows(start, j) for j in range(SUB)])
    solved = solve_block(d, solved)
    out = [list(r) for r in rows]
    for step in range(1, blocks):
        i = (pivot + step) % blocks
        for m in range(count):
            total = along_lanes(rows[m][i], lane0 + SUB - 1) * solved[m][SUB - 1]
            for j in range(SUB - 2, -1, -1):
                total = total + along_lanes(rows[m][i], lane0 + j) * solved[m][j]
            out[m][i] = jnp.where(here, 0.0, rows[m][i]) - total
    for m in range(count):
        packed = solved[m][0]
        for j in range(1, SUB):
            packed = jnp.where(sub == j, solved[m][j], packed)
        out[m][pivot] = packed
    return out


def invert(refs, panel_refs):
    size = refs[0].shape[0]
    count = len(refs)
    panel = size if count == 1 else min(32, size)
    blocks = panel // SUB
    sub = lax.broadcasted_iota(jnp.int32, (SUB, size), 0)
    lane = lax.broadcasted_iota(jnp.int32, (SUB, size), 1)
    wide = lax.broadcasted_iota(jnp.int32, (size, size), 1)
    if panel < size:
        for m in range(count):
            panel_refs[m][...] = jnp.zeros((size, size), f32)
    for p in range(size // panel):
        first = p * panel
        rows = [
            [refs[m][first + SUB * i:first + SUB * (i + 1), :] for i in range(blocks)]
            for m in range(count)
        ]
        for q in range(blocks):
            rows = sweep(rows, q, first + SUB * q, sub, lane)
        if panel < size:
            for m in range(count):
                if p > 0:
                    panel_refs[m][first - panel:first, :] = jnp.zeros((panel, size), f32)
                for i in range(blocks):
                    panel_refs[m][first + SUB * i:first + SUB * (i + 1), :] = rows[m][i]
            old = [refs[m][...] for m in range(count)]
            change = [dot_hi(old[m], panel_refs[m][...]) for m in range(count)]
            here = (wide >= first) & (wide < first + panel)
            for m in range(count):
                refs[m][...] = jnp.where(here, 0.0, old[m]) - change[m]
        for m in range(count):
            for i in range(blocks):
                refs[m][first + SUB * i:first + SUB * (i + 1), :] = rows[m][i]


def diagonal(row):
    size = row.shape[1]
    rows = lax.broadcasted_iota(jnp.int32, (size, size), 0)
    columns = lax.broadcasted_iota(jnp.int32, (size, size), 1)
    return jnp.where(rows == columns, row, 0.0)


def gram_row(basis_ref, turned_ref, pairs, tier, node_count):
    turned = turned_ref[tier].astype(f32)
    knots = turned.shape[0]
    blocks = []
    for other in range(tier + 1):
        index = pair_index(tier, other)
        high, low = zip(*[split(turned * pairs[n][index:index + 1, :]) for n in range(node_count)])
        both = dot(jnp.concatenate(high + low, axis=0), basis_ref[other])
        blocks.append(both[:node_count * knots] + both[node_count * knots:])
    return jnp.concatenate(blocks, axis=1)


def tree_kernel(basis_ref, turned_ref, prior_ref, *refs, top):
    tier_count, _, knots = basis_ref.shape
    leaves = 2 ** (tier_count - 1 - top)
    tiers = list(range(tier_count - 1, top - 1, -1))
    slot_refs, refs = refs[:leaves], refs[leaves:]
    inverse_refs, refs = refs[:len(tiers)], refs[len(tiers):]
    coupling_refs, refs = refs[:len(tiers)], refs[len(tiers):]
    rest_ref, panel_ref = refs

    pairs = [ref[...] for ref in slot_refs]
    kept = []
    for depth, tier in enumerate(tiers):
        nodes = len(pairs)
        width = tier * knots
        rows = gram_row(basis_ref, turned_ref, pairs, tier, nodes)
        rows = [rows[n * knots:(n + 1) * knots] for n in range(nodes)]
        for below, (row_list, coupling_list) in enumerate(kept):
            share = len(row_list) // nodes
            for n in range(nodes):
                for c in range(n * share, (n + 1) * share):
                    rows[n] = rows[n] - dot_tn(
                        row_list[c][:, width:width + knots], coupling_list[c][:, :width + knots]
                    )
        prior = diagonal(prior_ref[tier:tier + 1, :])
        inverse_ref = inverse_refs[depth]
        for n in range(nodes):
            inverse_ref[n] = rows[n][:, width:] + prior
        invert(
            [inverse_ref.at[n] for n in range(nodes)], [panel_ref.at[n] for n in range(nodes)]
        )
        couplings = [dot_hi(inverse_ref[n], rows[n][:, :width]) for n in range(nodes)]
        for n in range(nodes):
            coupling_refs[depth][n] = couplings[n]
        kept.append((rows, couplings))
        pairs = [pairs[2 * n] + pairs[2 * n + 1] for n in range(nodes // 2)] if nodes > 1 else pairs
    total = pairs[0]
    width = top * knots
    for tier in range(top):
        part = gram_row(basis_ref, turned_ref, [total], tier, 1)
        size = (tier + 1) * knots
        for row_list, coupling_list in kept:
            for row, coupling in zip(row_list, coupling_list):
                part = part - dot_tn(row[:, tier * knots:size], coupling[:, :size])
        rest_ref[tier * knots:size, :size] = part
        if size < width:
            rest_ref[tier * knots:size, size:] = jnp.zeros((knots, width - size), f32)


def tree(slots, basis_table, turned, prior_precision, top):
    tier_count, _, knots = basis_table.shape
    tiers = list(range(tier_count - 1, top - 1, -1))
    shapes = [(2 ** (tier - top), knots, knots) for tier in tiers]
    shapes += [(2 ** (tier - top), knots, tier * knots) for tier in tiers]
    shapes.append((top * knots, top * knots))
    out = pl.pallas_call(
        functools.partial(tree_kernel, top=top),
        in_specs=[vmem] * (3 + len(slots)),
        out_specs=[vmem] * len(shapes),
        out_shape=[jax.ShapeDtypeStruct(shape, f32) for shape in shapes],
        scratch_shapes=[pltpu.VMEM((len(slots), knots, knots), f32)],
        compiler_params=pltpu.CompilerParams(vmem_limit_bytes=48 * 2**20),
        cost_estimate=pl.CostEstimate(
            flops=40 * 10**9, bytes_accessed=4 * 2**20, transcendentals=0
        ),
        name="tree",
    )(basis_table, turned, prior_precision, *slots)
    count = len(tiers)
    return out[:count], out[count:2 * count], out[-1]


def forward_kernel(*refs, leaves):
    slot_refs, refs = refs[:leaves], refs[leaves:]
    out_refs = refs[-2:]
    coupling_refs = refs[:-2]
    knots = coupling_refs[0].shape[1]
    current = [ref[...] for ref in slot_refs]
    own = []
    for ref in coupling_refs:
        width = ref.shape[2]
        own.append(current[0][:, width:width + knots])
        reduced = [
            c[:, :width] - dot_hi(c[:, width:width + knots], ref[n]) for n, c in enumerate(current)
        ]
        current = (
            [reduced[2 * n] + reduced[2 * n + 1] for n in range(len(reduced) // 2)]
            if len(reduced) > 1 else reduced
        )
    out_refs[0][...] = current[0]
    out_refs[1][...] = jnp.concatenate(own, axis=1)


def forward(slots, couplings):
    fields = slots[0].shape[0]
    knots, width = couplings[-1].shape[1:]
    return pl.pallas_call(
        functools.partial(forward_kernel, leaves=len(slots)),
        in_specs=[vmem] * (len(slots) + len(couplings)),
        out_specs=[vmem] * 2,
        out_shape=[
            jax.ShapeDtypeStruct((fields, width), f32),
            jax.ShapeDtypeStruct((fields, knots * len(couplings)), f32),
        ],
        compiler_params=pltpu.CompilerParams(vmem_limit_bytes=32 * 2**20),
        name="forward",
    )(*slots, *couplings)


def top_kernel(*refs):
    rest_ref, other_ref, prior_ref, inverse_ref, coupling_ref, schur_ref = refs
    knots = inverse_ref.shape[0]
    total = rest_ref[...] + other_ref[...]
    row = total[knots:]
    inverse_ref[...] = row[:, knots:] + diagonal(prior_ref[1:2, :])
    invert([inverse_ref], [None])
    coupling = dot_hi(inverse_ref[...], row[:, :knots])
    coupling_ref[...] = coupling
    schur_ref[...] = total[:knots, :knots] - dot_tn(row[:, :knots], coupling)


def top_tier(rest, other, prior_precision, knots):
    return pl.pallas_call(
        top_kernel,
        in_specs=[vmem] * 3,
        out_specs=[vmem] * 3,
        out_shape=[jax.ShapeDtypeStruct((knots, knots), f32)] * 3,
        name="top_tier",
    )(rest, other, prior_precision)


def root_kernel(schur_ref, prior_ref, inverse_ref):
    inverse_ref[...] = schur_ref[...] + diagonal(prior_ref[0:1, :])
    invert([inverse_ref], [None])


def root_tier(schur, prior_precision):
    return pl.pallas_call(
        root_kernel,
        in_specs=[vmem] * 2,
        out_specs=vmem,
        out_shape=jax.ShapeDtypeStruct(schur.shape, f32),
        name="root_tier",
    )(schur, prior_precision)


def backward_kernel(*refs):
    out_ref, refs = refs[-1], refs[:-1]
    right_ref, root_inverse_ref, top_right_ref, top_inverse_ref, top_coupling_ref = refs[:5]
    own_ref, refs = refs[5], refs[6:]
    count = len(refs) // 2
    knots = root_inverse_ref.shape[0]
    path = dot_hi(right_ref[...], root_inverse_ref[...])
    local = dot_hi(top_right_ref[...], top_inverse_ref[...])
    path = jnp.concatenate(
        [path, local - dot_nt(path, top_coupling_ref[...], highest)], axis=1
    )
    for depth in range(count - 1, -1, -1):
        own = own_ref[:, depth * knots:(depth + 1) * knots]
        local = dot_hi(own, refs[depth][0])
        path = jnp.concatenate(
            [path, local - dot_nt(path, refs[count + depth][0], highest)], axis=1
        )
    out_ref[...] = path


def backward(right, root_inverse, top_right, top_inverse, top_coupling, own, inverses, couplings):
    fields = right.shape[0]
    width = couplings[0].shape[2] + couplings[0].shape[1]
    args = (right, root_inverse, top_right, top_inverse, top_coupling, own, *inverses, *couplings)
    return pl.pallas_call(
        backward_kernel,
        in_specs=[vmem] * len(args),
        out_specs=vmem,
        out_shape=jax.ShapeDtypeStruct((fields, width), f32),
        compiler_params=pltpu.CompilerParams(vmem_limit_bytes=32 * 2**20),
        name="backward",
    )(*args)


def fitted_kernel(pattern_ref, amplitude_ref, weight_ref, turned_ref, out_ref, table):
    tier_count, knots, pattern_count = turned_ref.shape
    field_count = weight_ref.shape[0]

    @pl.when(pl.program_id(0) == 0)
    def _():
        for tier in range(tier_count):
            high, low = split(weight_ref[:, tier * knots:(tier + 1) * knots])
            table[tier * field_count:(tier + 1) * field_count, :] = (
                dot(high, turned_ref[tier]) + dot(low, turned_ref[tier])
            ).astype(bf16)

    picked = dot(table[...], one_hot(pattern_ref[...], pattern_count))
    amp = amplitude_ref[...]
    total = picked[:field_count] * amp[0:1]
    for tier in range(1, tier_count):
        total = total + picked[tier * field_count:(tier + 1) * field_count] * amp[tier:tier + 1]
    out_ref[...] = total


def fitted_fields(pattern, amplitude, weights, turned):
    tier_count, knots, pattern_count = turned.shape
    obs = pattern.shape[0]
    field_count = weights.shape[0]
    block = min(2048, obs)
    return pl.pallas_call(
        fitted_kernel,
        grid=(obs // block,),
        in_specs=[
            pl.BlockSpec((1, block), lambda i: (0, i)),
            pl.BlockSpec((tier_count, block), lambda i: (0, i)),
            pl.BlockSpec(weights.shape, lambda i: (0, 0)),
            pl.BlockSpec(turned.shape, lambda i: (0, 0, 0)),
        ],
        out_specs=pl.BlockSpec((field_count, block), lambda i: (0, i)),
        out_shape=jax.ShapeDtypeStruct((field_count, obs), f32),
        scratch_shapes=[pltpu.VMEM((tier_count * field_count, pattern_count), bf16)],
        compiler_params=pltpu.CompilerParams(vmem_limit_bytes=48 * 2**20),
        name="fitted_fields",
    )(pattern.reshape(1, obs), amplitude, weights, turned)


def swapped(value, axis, mask):
    pairs = [(source, source ^ mask) for source in range(lax.axis_size(axis))]
    return lax.ppermute(value, axis, pairs)


def sum_over(value, axis, first_mask, size):
    mask = first_mask
    while mask < size:
        value = value + swapped(value, axis, mask)
        mask *= 2
    return value


def gather_half(value, leaves):
    region_count, obs_count = lax.axis_size("region"), lax.axis_size("obs")
    half = leaves // 2
    slots = []
    for offset in range(half):
        pairs = []
        for region in range(region_count):
            for obs in range(obs_count):
                mine = (region % leaves) // half
                source = region - region % leaves + (obs % 2) * half + (region % half ^ offset)
                source_obs = obs if mine == obs % 2 else obs ^ 1
                pairs.append((source * obs_count + source_obs, region * obs_count + obs))
        slots.append(lax.ppermute(value, ("region", "obs"), pairs))
    return slots


def spread_weights(weights, leaves):
    region_count, obs_count = lax.axis_size("region"), lax.axis_size("obs")
    half = leaves // 2
    field_count, width = weights.shape
    parts = obs_count // 2
    obs = lax.axis_index("obs")
    region = lax.axis_index("region")
    match = (region % leaves) // half == obs % 2
    place = obs // 2
    got = []
    for core in range(2):
        for offset in range(parts):
            if core == 0 and offset == 0:
                continue
            pairs = []
            for r in range(region_count):
                holder = (r % leaves) // half
                for part in range(parts):
                    source = r * obs_count + part * 2 + holder
                    target = r * obs_count + (part ^ offset) * 2 + (holder ^ core)
                    pairs.append((source, target))
            got.append(((core, offset), lax.ppermute(weights, ("region", "obs"), pairs)))
    got = dict(got)
    own = [
        jnp.where(match, weights if offset == 0 else got[0, offset], got[1, offset])
        for offset in range(parts)
    ]
    blocks = []
    for part in range(parts):
        value = own[0]
        for offset in range(1, parts):
            value = jnp.where(place ^ offset == part, own[offset], value)
        blocks.append(value)
    return jnp.concatenate(blocks, axis=0)


def shards(pattern, amplitude, basis_table, fields, prior_precision):
    tier_count, _, knots = basis_table.shape
    region_count, obs_count = lax.axis_size("region"), lax.axis_size("obs")
    leaves = 2 ** (tier_count - 2)
    field_count = fields.shape[0]
    parts = obs_count // 2
    part_fields = field_count // parts
    place = lax.axis_index("obs") // 2

    turned = jnp.swapaxes(basis_table, 1, 2)
    pairs, project = statistics(pattern, amplitude, fields, basis_table)
    pairs = sum_over(pairs, "obs", 1, obs_count)
    pair_slots = gather_half(pairs, leaves)

    mine = lax.dynamic_slice_in_dim(project, place * part_fields, part_fields, 0)
    total = mine
    for offset in range(1, parts):
        other = lax.dynamic_slice_in_dim(project, (place ^ offset) * part_fields, part_fields, 0)
        total = total + swapped(other, "obs", 2 * offset)
    total = total + swapped(total, "obs", 1)
    project_slots = gather_half(total, leaves)

    inverses, couplings, rest = tree(pair_slots, basis_table, turned, prior_precision, 2)
    other_rest = swapped(rest, "obs", 1)
    right, own = forward(project_slots, couplings)
    right = right + swapped(right, "obs", 1)
    top_inverse, top_coupling, schur = top_tier(rest, other_rest, prior_precision, knots)
    top_right = right[:, knots:]
    root_right = right[:, :knots] - jnp.dot(top_right, top_coupling, precision=highest)
    schur = sum_over(schur, "region", leaves, region_count)
    root_right = sum_over(root_right, "region", leaves, region_count)
    root_inverse = root_tier(schur, prior_precision)
    weights = backward(
        root_right, root_inverse, top_right, top_inverse, top_coupling, own, inverses, couplings
    )
    weights = spread_weights(weights, leaves)
    return fitted_fields(pattern, amplitude, weights, turned)


def solution(mesh):
    return jax.shard_map(
        shards,
        mesh=mesh,
        in_specs=(
            P(("region", "obs")),
            P(None, ("region", "obs")),
            P(),
            P(None, ("region", "obs")),
            P(),
        ),
        out_specs=P(None, ("region", "obs")),
        check_vma=False,
    )
```

```python
import functools

import jax
import jax.numpy as jnp
from jax import lax
from jax.experimental import pallas as pl
from jax.experimental.pallas import tpu as pltpu
from jax.sharding import PartitionSpec as P

highest = lax.Precision.HIGHEST
f32 = jnp.float32
bf16 = jnp.bfloat16
SUB = 8
vmem = pl.BlockSpec(memory_space=pltpu.VMEM)


def pair_index(tier, other):
    return tier * (tier + 1) // 2 + other


def dot(a, b):
    return jnp.dot(a, b, preferred_element_type=f32)


def dot_nt(a, b, precision=None):
    return lax.dot_general(
        a, b, (((1,), (1,)), ((), ())), precision=precision, preferred_element_type=f32
    )


def dot_tn(a, b):
    return lax.dot_general(
        a, b, (((0,), (0,)), ((), ())), precision=highest, preferred_element_type=f32
    )


def dot_hi(a, b):
    return jnp.dot(a, b, precision=highest, preferred_element_type=f32)


def split(value):
    high = value.astype(bf16)
    return high, (value - high.astype(f32)).astype(bf16)


def one_hot(pattern_row, pattern_count):
    rows = lax.broadcasted_iota(jnp.int16, (pattern_count, pattern_row.shape[1]), 0)
    return jnp.where(rows == pattern_row.astype(jnp.int16), jnp.asarray(1, bf16), jnp.asarray(0, bf16))


def stats_kernel(pattern_ref, amplitude_ref, fields_ref, basis_ref, pairs_ref, project_ref,
                 prods, acc):
    step = pl.program_id(0)
    tier_count, pattern_count, knots = basis_ref.shape
    field_count = fields_ref.shape[0]
    pair_rows = prods.shape[0]
    amp = amplitude_ref[...]
    prods[...] = jnp.zeros_like(prods)
    for tier in range(tier_count):
        first = pair_index(tier, 0)
        prods[first:first + tier + 1, :] = amp[:tier + 1] * amp[tier:tier + 1]
    pair_high, pair_low = split(prods[...])
    plain = fields_ref[...]
    field_rows = plain.astype(f32)
    shifted = amp - 1.0
    values = jnp.concatenate(
        [pair_high, pair_low, plain]
        + [(field_rows * shifted[tier:tier + 1]).astype(bf16) for tier in range(tier_count)],
        axis=0,
    )
    part = dot_nt(values, one_hot(pattern_ref[...], pattern_count))

    @pl.when(step == 0)
    def _():
        acc[...] = part

    @pl.when(step > 0)
    def _():
        acc[...] += part

    @pl.when(step == pl.num_programs(0) - 1)
    def _():
        pairs_ref[...] = acc[:pair_rows] + acc[pair_rows:2 * pair_rows]
        base = 2 * pair_rows
        plain_sum = acc[base:base + field_count]
        for tier in range(tier_count):
            first = base + (tier + 1) * field_count
            high, low = split(plain_sum + acc[first:first + field_count])
            project_ref[:, tier * knots:(tier + 1) * knots] = (
                dot(high, basis_ref[tier]) + dot(low, basis_ref[tier])
            )


def statistics(pattern, amplitude, fields, basis_table):
    tier_count, pattern_count, knots = basis_table.shape
    field_count, obs = fields.shape
    block = min(4096, obs)
    pair_rows = -(-pair_index(tier_count, 0) // 16) * 16
    rows = 2 * pair_rows + (1 + tier_count) * field_count
    return pl.pallas_call(
        stats_kernel,
        grid=(obs // block,),
        in_specs=[
            pl.BlockSpec((1, block), lambda i: (0, i)),
            pl.BlockSpec((tier_count, block), lambda i: (0, i)),
            pl.BlockSpec((field_count, block), lambda i: (0, i)),
            pl.BlockSpec(basis_table.shape, lambda i: (0, 0, 0)),
        ],
        out_specs=[
            pl.BlockSpec((pair_rows, pattern_count), lambda i: (0, 0)),
            pl.BlockSpec((field_count, tier_count * knots), lambda i: (0, 0)),
        ],
        out_shape=[
            jax.ShapeDtypeStruct((pair_rows, pattern_count), f32),
            jax.ShapeDtypeStruct((field_count, tier_count * knots), f32),
        ],
        scratch_shapes=[
            pltpu.VMEM((pair_rows, block), f32),
            pltpu.VMEM((rows, pattern_count), f32),
        ],
        compiler_params=pltpu.CompilerParams(vmem_limit_bytes=58 * 2**20),
        cost_estimate=pl.CostEstimate(
            flops=2 * rows * pattern_count * obs, bytes_accessed=4 * 2**20, transcendentals=0
        ),
        name="statistics",
    )(pattern.reshape(1, obs), amplitude, fields, basis_table)


def along_rows(x, row):
    return jnp.broadcast_to(x[row:row + 1, :], x.shape)


def along_lanes(x, lane):
    return jnp.broadcast_to(x[:, lane:lane + 1], x.shape)


def tree_sum(values):
    while len(values) > 1:
        ends = values[len(values) - len(values) % 2:]
        values = [values[i] + values[i + 1] for i in range(0, len(values) - 1, 2)] + ends
    return values[0]


def sweep(rows, first, group, lane0, sub, lane):
    count, blocks, size = len(rows), len(rows[0]), SUB * group
    here = (lane >= lane0) & (lane < lane0 + size)
    columns, pivot = [], []
    for m in range(count):
        block = rows[m][first:first + group]
        columns.append([[along_lanes(b, lane0 + j) for b in block] for j in range(size)])
        pivot.append([
            jnp.where(here, (lane - lane0 - SUB * a == sub).astype(f32), b)
            for a, b in enumerate(block)
        ])
    for k in range(size):
        at, row = divmod(k, SUB)
        is_row = sub == row
        scale = [
            pltpu.reciprocal(along_rows(columns[m][k][at], row), approx=True) for m in range(count)
        ]

        def eliminated(parts, m):
            scaled = along_rows(parts[at], row) * scale[m]
            out = [part - c * scaled for part, c in zip(parts, columns[m][k])]
            out[at] = jnp.where(is_row, scaled, out[at])
            return out

        for j in range(k + 1, size):
            for m in range(count):
                columns[m][j] = eliminated(columns[m][j], m)
        for m in range(count):
            pivot[m] = eliminated(pivot[m], m)
    solved = [[along_rows(pivot[m][j // SUB], j % SUB) for j in range(size)] for m in range(count)]
    out = [list(r) for r in rows]
    for step in range(blocks - group):
        i = (first + group + step) % blocks
        for m in range(count):
            total = tree_sum([along_lanes(rows[m][i], lane0 + j) * solved[m][j] for j in range(size)])
            out[m][i] = jnp.where(here, 0.0, rows[m][i]) - total
    for m in range(count):
        out[m][first:first + group] = pivot[m]
    return out


def invert(refs, panel_refs):
    size = refs[0].shape[0]
    count = len(refs)
    panel, group = (min(64, size), 2) if count <= 2 else (min(32, size), 1)
    blocks = panel // SUB
    sub = lax.broadcasted_iota(jnp.int32, (SUB, size), 0)
    lane = lax.broadcasted_iota(jnp.int32, (SUB, size), 1)
    wide = lax.broadcasted_iota(jnp.int32, (size, size), 1)
    for m in range(count):
        panel_refs[m][...] = jnp.zeros((size, size), f32)
    for p in range(size // panel):
        first = p * panel
        rows = [
            [refs[m][first + SUB * i:first + SUB * (i + 1), :] for i in range(blocks)]
            for m in range(count)
        ]
        for q in range(0, blocks, group):
            rows = sweep(rows, q, group, first + SUB * q, sub, lane)
        for m in range(count):
            if p > 0:
                panel_refs[m][first - panel:first, :] = jnp.zeros((panel, size), f32)
            for i in range(blocks):
                panel_refs[m][first + SUB * i:first + SUB * (i + 1), :] = rows[m][i]
        old = [refs[m][...] for m in range(count)]
        change = [dot_hi(old[m], panel_refs[m][...]) for m in range(count)]
        here = (wide >= first) & (wide < first + panel)
        for m in range(count):
            refs[m][...] = jnp.where(here, 0.0, old[m]) - change[m]
            for i in range(blocks):
                refs[m][first + SUB * i:first + SUB * (i + 1), :] = rows[m][i]


def diagonal(row):
    size = row.shape[1]
    rows = lax.broadcasted_iota(jnp.int32, (size, size), 0)
    columns = lax.broadcasted_iota(jnp.int32, (size, size), 1)
    return jnp.where(rows == columns, row, 0.0)


def gram_row(basis_ref, turned_ref, pairs, tier, node_count):
    turned = turned_ref[tier].astype(f32)
    knots = turned.shape[0]
    blocks = []
    for other in range(tier + 1):
        index = pair_index(tier, other)
        high, low = zip(*[split(turned * pairs[n][index:index + 1, :]) for n in range(node_count)])
        both = dot(jnp.concatenate(high + low, axis=0), basis_ref[other])
        blocks.append(both[:node_count * knots] + both[node_count * knots:])
    return jnp.concatenate(blocks, axis=1)


def eliminate(rows, tier, lower, prior_ref, inverse_ref, coupling_ref, panel_ref):
    knots = prior_ref.shape[1]
    width = tier * knots
    nodes = len(rows)
    prior = diagonal(prior_ref[tier:tier + 1, :])
    for n in range(nodes):
        inverse_ref[n] = rows[n][:, width:] + prior
    invert([inverse_ref.at[n] for n in range(nodes)], [panel_ref.at[n] for n in range(nodes)])
    couplings = [dot_hi(inverse_ref[n], rows[n][:, :width]) for n in range(nodes)]
    for n in range(nodes):
        coupling_ref[n] = couplings[n]
    for below in range(tier - 1, -1, -1):
        share = nodes // len(lower[below])
        first, last = below * knots, (below + 1) * knots
        for n in range(nodes):
            lower[below][n // share] -= dot_tn(rows[n][:, first:last], couplings[n][:, :last])


def store_rest(rest_ref, lower, top):
    knots = rest_ref.shape[0] // top
    for tier in range(top):
        size = (tier + 1) * knots
        rest_ref[size - knots:size, :size] = lower[tier][0]
        if tier < top - 1:
            rest_ref[size - knots:size, size:] = jnp.zeros((knots, (top - 1 - tier) * knots), f32)


def leaf_kernel(basis_ref, turned_ref, prior_ref, *refs, top):
    tier = basis_ref.shape[0] - 1
    leaves = 2 ** (tier - top)
    slot_refs, refs = refs[:leaves], refs[leaves:]
    inverse_ref, coupling_ref, rest_ref, panel_ref = refs[0], refs[1], refs[-2], refs[-1]
    row_refs = refs[2:-2]
    knots = basis_ref.shape[2]
    pairs = [ref[...] for ref in slot_refs]
    rows = gram_row(basis_ref, turned_ref, pairs, tier, leaves)
    lower = {}
    for below in range(tier - 1, -1, -1):
        if len(pairs) > 1:
            pairs = [pairs[2 * n] + pairs[2 * n + 1] for n in range(len(pairs) // 2)]
        part = gram_row(basis_ref, turned_ref, pairs, below, len(pairs))
        lower[below] = [part[n * knots:(n + 1) * knots] for n in range(len(pairs))]
    rows = [rows[n * knots:(n + 1) * knots] for n in range(leaves)]
    eliminate(rows, tier, lower, prior_ref, inverse_ref, coupling_ref, panel_ref)
    for ref, below in zip(row_refs, range(tier - 1, top - 1, -1)):
        for n, value in enumerate(lower[below]):
            ref[n] = value
    store_rest(rest_ref, lower, top)


def inner_kernel(*refs, top, count):
    row_refs, (rest_in, prior_ref), refs = refs[:count], refs[count:count + 2], refs[count + 2:]
    inverse_refs, coupling_refs, (rest_ref, panel_ref) = refs[:count], refs[count:-2], refs[-2:]
    knots = prior_ref.shape[1]
    lower = {
        top + count - 1 - i: [ref[n] for n in range(ref.shape[0])]
        for i, ref in enumerate(row_refs)
    }
    for tier in range(top):
        size = (tier + 1) * knots
        lower[tier] = [rest_in[size - knots:size, :size]]
    for i in range(count):
        tier = top + count - 1 - i
        eliminate(
            lower[tier], tier, lower, prior_ref, inverse_refs[i], coupling_refs[i], panel_ref
        )
    store_rest(rest_ref, lower, top)


def whole_call(kernel, args, shapes, scratch, name, limit=8, flops=10**10):
    return pl.pallas_call(
        kernel,
        in_specs=[vmem] * len(args),
        out_specs=[vmem] * len(shapes),
        out_shape=[jax.ShapeDtypeStruct(shape, f32) for shape in shapes],
        scratch_shapes=[pltpu.VMEM(shape, f32) for shape in scratch],
        compiler_params=pltpu.CompilerParams(vmem_limit_bytes=limit * 2**20),
        cost_estimate=pl.CostEstimate(flops=flops, bytes_accessed=2**20, transcendentals=0),
        name=name,
    )(*args)


def leaf_tier(slots, basis_table, turned, prior_precision, top):
    tier_count, _, knots = basis_table.shape
    tier = tier_count - 1
    leaves = len(slots)
    shapes = [(leaves, knots, knots), (leaves, knots, tier * knots)]
    shapes += [(2 ** (t - top), knots, (t + 1) * knots) for t in range(tier - 1, top - 1, -1)]
    shapes.append((top * knots, top * knots))
    inverse, coupling, *rows, rest = whole_call(
        functools.partial(leaf_kernel, top=top),
        (basis_table, turned, prior_precision, *slots),
        shapes, [(leaves, knots, knots)], "leaf_tier", limit=16, flops=2 * 10**10,
    )
    return inverse, coupling, rows, rest


def inner_tiers(rows, rest, prior_precision, top):
    knots = prior_precision.shape[1]
    count = len(rows)
    nodes = [value.shape[0] for value in rows]
    shapes = [(n, knots, knots) for n in nodes]
    shapes += [(n, knots, value.shape[2] - knots) for n, value in zip(nodes, rows)]
    shapes.append(rest.shape)
    out = whole_call(
        functools.partial(inner_kernel, top=top, count=count),
        (*rows, rest, prior_precision),
        shapes, [(max(nodes), knots, knots)], "inner_tiers", limit=16, flops=2 * 10**10,
    )
    return list(out[:count]), list(out[count:-1]), out[-1]


def forward_kernel(*refs, leaves):
    slot_refs, refs = refs[:leaves], refs[leaves:]
    out_refs = refs[-2:]
    coupling_refs = refs[:-2]
    knots = coupling_refs[0].shape[1]
    current = [ref[...] for ref in slot_refs]
    own = []
    for ref in coupling_refs:
        width = ref.shape[2]
        own.append(current[0][:, width:width + knots])
        reduced = [
            c[:, :width] - dot_hi(c[:, width:width + knots], ref[n]) for n, c in enumerate(current)
        ]
        current = (
            [reduced[2 * n] + reduced[2 * n + 1] for n in range(len(reduced) // 2)]
            if len(reduced) > 1 else reduced
        )
    out_refs[0][...] = current[0]
    out_refs[1][...] = jnp.concatenate(own, axis=1)


def forward(slots, couplings):
    fields = slots[0].shape[0]
    knots, width = couplings[-1].shape[1:]
    return pl.pallas_call(
        functools.partial(forward_kernel, leaves=len(slots)),
        in_specs=[vmem] * (len(slots) + len(couplings)),
        out_specs=[vmem] * 2,
        out_shape=[
            jax.ShapeDtypeStruct((fields, width), f32),
            jax.ShapeDtypeStruct((fields, knots * len(couplings)), f32),
        ],
        compiler_params=pltpu.CompilerParams(vmem_limit_bytes=8 * 2**20),
        name="forward",
    )(*slots, *couplings)


def top_step(rest, other, right, other_right, prior_row, inverse_ref, panel_ref):
    knots = inverse_ref.shape[0]
    total = rest + other
    right = right + other_right
    row = total[knots:]
    inverse_ref[...] = row[:, knots:] + diagonal(prior_row)
    invert([inverse_ref], [panel_ref])
    coupling = dot_hi(inverse_ref[...], row[:, :knots])
    schur = total[:knots, :knots] - dot_tn(row[:, :knots], coupling)
    top_right = right[:, knots:]
    return coupling, schur, top_right, right[:, :knots] - dot_hi(top_right, coupling)


def root_step(schur, root_right, prior_row, inverse_ref, panel_ref):
    inverse_ref[...] = schur + diagonal(prior_row)
    invert([inverse_ref], [panel_ref])
    return dot_hi(root_right, inverse_ref[...])


def path_step(path, right, inverse, coupling):
    local = dot_hi(right, inverse) - dot_nt(path, coupling, highest)
    return jnp.concatenate([path, local], axis=1)


def descend(path, own_ref, refs):
    count = len(refs) // 2
    knots = refs[0].shape[1]
    for depth in range(count - 1, -1, -1):
        own = own_ref[:, depth * knots:(depth + 1) * knots]
        path = path_step(path, own, refs[depth][0], refs[count + depth][0])
    return path


def both_kernel(*refs):
    rest_ref, other_ref, right_ref, other_right_ref, prior_ref, own_ref = refs[:6]
    refs, (out_ref, top_ref, root_ref, panel_ref) = refs[6:-4], refs[-4:]
    coupling, schur, top_right, root_right = top_step(
        rest_ref[...], other_ref[...], right_ref[...], other_right_ref[...], prior_ref[1:2, :],
        top_ref, panel_ref,
    )
    path = root_step(schur, root_right, prior_ref[0:1, :], root_ref, panel_ref)
    path = path_step(path, top_right, top_ref[...], coupling)
    out_ref[...] = descend(path, own_ref, refs)


def top_kernel(*refs):
    rest_ref, other_ref, right_ref, other_right_ref, prior_ref = refs[:5]
    inverse_ref, coupling_ref, schur_ref, top_right_ref, root_right_ref, panel_ref = refs[5:]
    coupling_ref[...], schur_ref[...], top_right_ref[...], root_right_ref[...] = top_step(
        rest_ref[...], other_ref[...], right_ref[...], other_right_ref[...], prior_ref[1:2, :],
        inverse_ref, panel_ref,
    )


def root_kernel(*refs):
    schur_ref, root_right_ref, prior_ref, top_inverse_ref, top_coupling_ref = refs[:5]
    top_right_ref, own_ref = refs[5:7]
    refs, (out_ref, root_ref, panel_ref) = refs[7:-3], refs[-3:]
    path = root_step(
        schur_ref[...], root_right_ref[...], prior_ref[0:1, :], root_ref, panel_ref
    )
    path = path_step(path, top_right_ref[...], top_inverse_ref[...], top_coupling_ref[...])
    out_ref[...] = descend(path, own_ref, refs)


def path_weights(rest, right, own, prior_precision, inverses, couplings, leaves):
    knots = prior_precision.shape[1]
    fields = right.shape[0]
    square = (knots, knots)
    weight_shape = (fields, prior_precision.shape[0] * knots)
    region_count = lax.axis_size("region")
    ends = (rest, swapped(rest, "obs", 1), right, swapped(right, "obs", 1), prior_precision)
    if region_count == leaves:
        args = (*ends, own, *inverses, *couplings)
        return whole_call(both_kernel, args, [weight_shape], [square] * 3, "top_and_root")[0]
    shapes = [square] * 3 + [(fields, knots)] * 2
    inverse, coupling, schur, top_right, root_right = whole_call(
        top_kernel, ends, shapes, [square], "top"
    )
    schur = sum_over(schur, "region", leaves, region_count)
    root_right = sum_over(root_right, "region", leaves, region_count)
    args = (schur, root_right, prior_precision, inverse, coupling, top_right, own)
    args += (*inverses, *couplings)
    return whole_call(root_kernel, args, [weight_shape], [square] * 2, "root")[0]


def fitted_kernel(pattern_ref, amplitude_ref, weight_ref, turned_ref, out_ref, table):
    tier_count, knots, pattern_count = turned_ref.shape
    field_count = weight_ref.shape[0]

    @pl.when(pl.program_id(0) == 0)
    def _():
        for tier in range(tier_count):
            high, low = split(weight_ref[:, tier * knots:(tier + 1) * knots])
            table[tier * field_count:(tier + 1) * field_count, :] = (
                dot(high, turned_ref[tier]) + dot(low, turned_ref[tier])
            ).astype(bf16)

    picked = dot(table[...], one_hot(pattern_ref[...], pattern_count))
    amp = amplitude_ref[...]
    total = picked[:field_count] * amp[0:1]
    for tier in range(1, tier_count):
        total = total + picked[tier * field_count:(tier + 1) * field_count] * amp[tier:tier + 1]
    out_ref[...] = total


def fitted_fields(pattern, amplitude, weights, turned):
    tier_count, knots, pattern_count = turned.shape
    obs = pattern.shape[0]
    field_count = weights.shape[0]
    block = min(2048, obs)
    return pl.pallas_call(
        fitted_kernel,
        grid=(obs // block,),
        in_specs=[
            pl.BlockSpec((1, block), lambda i: (0, i)),
            pl.BlockSpec((tier_count, block), lambda i: (0, i)),
            pl.BlockSpec(weights.shape, lambda i: (0, 0)),
            pl.BlockSpec(turned.shape, lambda i: (0, 0, 0)),
        ],
        out_specs=pl.BlockSpec((field_count, block), lambda i: (0, i)),
        out_shape=jax.ShapeDtypeStruct((field_count, obs), f32),
        scratch_shapes=[pltpu.VMEM((tier_count * field_count, pattern_count), bf16)],
        compiler_params=pltpu.CompilerParams(vmem_limit_bytes=16 * 2**20),
        name="fitted_fields",
    )(pattern.reshape(1, obs), amplitude, weights, turned)


def swapped(value, axis, mask):
    pairs = [(source, source ^ mask) for source in range(lax.axis_size(axis))]
    return lax.ppermute(value, axis, pairs)


def sum_over(value, axis, first_mask, size):
    mask = first_mask
    while mask < size:
        value = value + swapped(value, axis, mask)
        mask *= 2
    return value


def in_own_half(leaves):
    return (lax.axis_index("region") % leaves) // (leaves // 2) == lax.axis_index("obs") % 2


def sum_for_half(value, leaves):
    region_count, obs_count = lax.axis_size("region"), lax.axis_size("obs")
    half = leaves // 2
    total = jnp.where(in_own_half(leaves), value, 0.0)
    for offset in range(obs_count // 2):
        pairs = []
        for region in range(region_count):
            for obs in range(obs_count):
                source = region * obs_count + obs
                if (region % leaves) // half != obs % 2:
                    pairs.append((source, (region ^ half) * obs_count + (obs ^ 1 ^ 2 * offset)))
                elif offset > 0:
                    pairs.append((source, region * obs_count + (obs ^ 2 * offset)))
        total = total + lax.ppermute(value, ("region", "obs"), pairs)
    return total


def gather_half(value, leaves):
    return [value] + [swapped(value, "region", offset) for offset in range(1, leaves // 2)]


def spread_weights(weights, leaves):
    region_count, obs_count = lax.axis_size("region"), lax.axis_size("obs")
    half = leaves // 2
    pairs = []
    for region in range(region_count):
        holder = (region % leaves) // half
        for obs in range(holder, obs_count, 2):
            source = region * obs_count + obs
            pairs.append((source, region * obs_count + (obs ^ 1)))
    other = lax.ppermute(weights, ("region", "obs"), pairs)
    return jnp.where(in_own_half(leaves), weights, other)


def shards(pattern, amplitude, basis_table, fields, prior_precision):
    tier_count = basis_table.shape[0]
    leaves = 2 ** (tier_count - 2)
    turned = jnp.swapaxes(basis_table, 1, 2)
    pairs, project = statistics(pattern, amplitude, fields, basis_table)
    pairs = pairs + swapped(pairs, "obs", 1)
    project = project + swapped(project, "obs", 1)
    pairs = sum_for_half(pairs, leaves)
    pair_slots = gather_half(pairs, leaves)
    pair_slots, project = lax.optimization_barrier((pair_slots, project))
    inverse, coupling, rows, rest = leaf_tier(pair_slots, basis_table, turned, prior_precision, 2)
    project = sum_for_half(project, leaves)
    rows, rest, project = lax.optimization_barrier((rows, rest, project))
    inverses, couplings, rest = inner_tiers(rows, rest, prior_precision, 2)
    inverses, couplings = [inverse] + inverses, [coupling] + couplings
    project_slots = gather_half(project, leaves)
    right, own = forward(project_slots, couplings)
    rest, right = lax.optimization_barrier((rest, right))
    weights = path_weights(rest, right, own, prior_precision, inverses, couplings, leaves)
    weights = spread_weights(weights, leaves)
    return fitted_fields(pattern, amplitude, weights, turned)


def solution(mesh):
    return jax.shard_map(
        shards,
        mesh=mesh,
        in_specs=(
            P(("region", "obs")),
            P(None, ("region", "obs")),
            P(),
            P(None, ("region", "obs")),
            P(),
        ),
        out_specs=P(None, ("region", "obs")),
        check_vma=False,
    )
```

```python
import functools

import jax
import jax.numpy as jnp
from jax import lax
from jax.experimental import pallas as pl
from jax.experimental.pallas import tpu as pltpu
from jax.sharding import PartitionSpec as P

highest = lax.Precision.HIGHEST
f32 = jnp.float32
bf16 = jnp.bfloat16
SUB = 8
vmem = pl.BlockSpec(memory_space=pltpu.VMEM)


def pair_index(tier, other):
    return tier * (tier + 1) // 2 + other


def dot(a, b):
    return jnp.dot(a, b, preferred_element_type=f32)


def dot_nt(a, b, precision=None):
    return lax.dot_general(
        a, b, (((1,), (1,)), ((), ())), precision=precision, preferred_element_type=f32
    )


def dot_tn(a, b):
    return lax.dot_general(
        a, b, (((0,), (0,)), ((), ())), precision=highest, preferred_element_type=f32
    )


def dot_hi(a, b):
    return jnp.dot(a, b, precision=highest, preferred_element_type=f32)


def split(value):
    high = value.astype(bf16)
    return high, (value - high.astype(f32)).astype(bf16)


def split3(value):
    high = value.astype(bf16)
    rest = value - high.astype(f32)
    middle = rest.astype(bf16)
    return high, middle, (rest - middle.astype(f32)).astype(bf16)


def one_hot(pattern_row, pattern_count):
    rows = lax.broadcasted_iota(jnp.int16, (pattern_count, pattern_row.shape[1]), 0)
    return jnp.where(rows == pattern_row.astype(jnp.int16), jnp.asarray(1, bf16), jnp.asarray(0, bf16))


def stats_kernel(pattern_ref, amplitude_ref, fields_ref, basis_ref, out_ref, prods, acc):
    step = pl.program_id(0)
    tier_count, pattern_count, knots = basis_ref.shape
    field_count = fields_ref.shape[0]
    pair_rows = prods.shape[0]
    amp = amplitude_ref[...]
    prods[...] = jnp.zeros_like(prods)
    for tier in range(tier_count):
        first = pair_index(tier, 0)
        prods[first:first + tier + 1, :] = amp[:tier + 1] * amp[tier:tier + 1]
    pair_parts = split3(prods[...])
    plain = fields_ref[...]
    field_rows = plain.astype(f32)
    shifted = amp - 1.0
    values = jnp.concatenate(
        [*pair_parts, plain]
        + [(field_rows * shifted[tier:tier + 1]).astype(bf16) for tier in range(tier_count)],
        axis=0,
    )
    part = dot_nt(values, one_hot(pattern_ref[...], pattern_count))

    @pl.when(step == 0)
    def _():
        acc[...] = part

    @pl.when(step > 0)
    def _():
        acc[...] += part

    @pl.when(step == pl.num_programs(0) - 1)
    def _():
        base = 3 * pair_rows
        out_ref[...] = jnp.zeros_like(out_ref)
        out_ref[:pair_rows, :pattern_count] = acc[:pair_rows] + (
            acc[pair_rows:2 * pair_rows] + acc[2 * pair_rows:base]
        )
        plain_sum = acc[base:base + field_count]
        for tier in range(tier_count):
            first = base + (tier + 1) * field_count
            high, low = split(plain_sum + acc[first:first + field_count])
            out_ref[pair_rows:, tier * knots:(tier + 1) * knots] = (
                dot(high, basis_ref[tier]) + dot(low, basis_ref[tier])
            )


def statistics(pattern, amplitude, fields, basis_table):
    tier_count, pattern_count, knots = basis_table.shape
    field_count, obs = fields.shape
    block = min(4096, obs)
    pair_rows = -(-pair_index(tier_count, 0) // 16) * 16
    rows = 3 * pair_rows + (1 + tier_count) * field_count
    width = max(pattern_count, tier_count * knots)
    return pl.pallas_call(
        stats_kernel,
        grid=(obs // block,),
        in_specs=[
            pl.BlockSpec((1, block), lambda i: (0, i)),
            pl.BlockSpec((tier_count, block), lambda i: (0, i)),
            pl.BlockSpec((field_count, block), lambda i: (0, i)),
            pl.BlockSpec(basis_table.shape, lambda i: (0, 0, 0)),
        ],
        out_specs=pl.BlockSpec((pair_rows + field_count, width), lambda i: (0, 0)),
        out_shape=pltpu.VMEM((pair_rows + field_count, width), f32),
        scratch_shapes=[
            pltpu.VMEM((pair_rows, block), f32),
            pltpu.VMEM((rows, pattern_count), f32),
        ],
        compiler_params=pltpu.CompilerParams(vmem_limit_bytes=58 * 2**20),
        cost_estimate=pl.CostEstimate(
            flops=2 * rows * pattern_count * obs, bytes_accessed=4 * 2**20, transcendentals=0
        ),
        name="statistics",
    )(pattern.reshape(1, obs), amplitude, fields, basis_table)


def along_rows(x, row):
    return jnp.broadcast_to(x[row:row + 1, :], x.shape)


def along_lanes(x, lane):
    return jnp.broadcast_to(x[:, lane:lane + 1], x.shape)


def tree_sum(values):
    while len(values) > 1:
        ends = values[len(values) - len(values) % 2:]
        values = [values[i] + values[i + 1] for i in range(0, len(values) - 1, 2)] + ends
    return values[0]


def sweep(rows, first, group, lane0, sub, lane):
    count, blocks, size = len(rows), len(rows[0]), SUB * group
    here = (lane >= lane0) & (lane < lane0 + size)
    columns, pivot = [], []
    for m in range(count):
        block = rows[m][first:first + group]
        columns.append([[along_lanes(b, lane0 + j) for b in block] for j in range(size)])
        pivot.append([
            jnp.where(here, (lane - lane0 - SUB * a == sub).astype(f32), b)
            for a, b in enumerate(block)
        ])
    for k in range(size):
        at, row = divmod(k, SUB)
        is_row = sub == row
        scale = [
            pltpu.reciprocal(along_rows(columns[m][k][at], row), approx=True) for m in range(count)
        ]

        def eliminated(parts, m):
            scaled = along_rows(parts[at], row) * scale[m]
            out = [part - c * scaled for part, c in zip(parts, columns[m][k])]
            out[at] = jnp.where(is_row, scaled, out[at])
            return out

        for j in range(k + 1, size):
            for m in range(count):
                columns[m][j] = eliminated(columns[m][j], m)
        for m in range(count):
            pivot[m] = eliminated(pivot[m], m)
    solved = [[along_rows(pivot[m][j // SUB], j % SUB) for j in range(size)] for m in range(count)]
    out = [list(r) for r in rows]
    for step in range(blocks - group):
        i = (first + group + step) % blocks
        for m in range(count):
            total = tree_sum([along_lanes(rows[m][i], lane0 + j) * solved[m][j] for j in range(size)])
            out[m][i] = jnp.where(here, 0.0, rows[m][i]) - total
    for m in range(count):
        out[m][first:first + group] = pivot[m]
    return out


def invert(refs, panel_refs, others=()):
    others = list(others)
    size = refs[0].shape[0]
    count = len(refs)
    panel, group = (min(64, size), 2) if count <= 2 else (min(32, size), 1)
    blocks = panel // SUB
    steps = size // (SUB * group)
    each = -(-len(others) // steps)
    sub = lax.broadcasted_iota(jnp.int32, (SUB, size), 0)
    lane = lax.broadcasted_iota(jnp.int32, (SUB, size), 1)
    wide = lax.broadcasted_iota(jnp.int32, (size, size), 1)
    for m in range(count):
        panel_refs[m][...] = jnp.zeros((size, size), f32)
    for p in range(size // panel):
        first = p * panel
        rows = [
            [refs[m][first + SUB * i:first + SUB * (i + 1), :] for i in range(blocks)]
            for m in range(count)
        ]
        for q in range(0, blocks, group):
            for work in others[:each]:
                work()
            others = others[each:]
            rows = sweep(rows, q, group, first + SUB * q, sub, lane)
        for m in range(count):
            if p > 0:
                panel_refs[m][first - panel:first, :] = jnp.zeros((panel, size), f32)
            for i in range(blocks):
                panel_refs[m][first + SUB * i:first + SUB * (i + 1), :] = rows[m][i]
        old = [refs[m][...] for m in range(count)]
        change = [dot_hi(old[m], panel_refs[m][...]) for m in range(count)]
        here = (wide >= first) & (wide < first + panel)
        for m in range(count):
            refs[m][...] = jnp.where(here, 0.0, old[m]) - change[m]
            for i in range(blocks):
                refs[m][first + SUB * i:first + SUB * (i + 1), :] = rows[m][i]


def diagonal(row):
    size = row.shape[1]
    rows = lax.broadcasted_iota(jnp.int32, (size, size), 0)
    columns = lax.broadcasted_iota(jnp.int32, (size, size), 1)
    return jnp.where(rows == columns, row, 0.0)


def gram_block(basis_ref, turned_ref, pairs, tier, other):
    turned = turned_ref[tier].astype(f32)
    index = pair_index(tier, other)
    parts = zip(*[split3(turned * pair[index:index + 1, :]) for pair in pairs])
    product = dot(jnp.concatenate(sum(parts, ()), axis=0), basis_ref[other])
    size = len(pairs) * turned.shape[0]
    return product[:size] + (product[size:2 * size] + product[2 * size:])


def update(target_ref, below, row_ref, coupling_ref):
    nodes, knots = row_ref.shape[:2]
    share = nodes // target_ref.shape[0]
    first, last = below * knots, (below + 1) * knots
    for n in range(target_ref.shape[0]):
        part = slice(n * share, (n + 1) * share)
        left = row_ref[part, :, first:last].reshape(share * knots, knots)
        right = coupling_ref[part, :, :last].reshape(share * knots, last)
        target_ref[n, :, :last] -= dot_tn(left, right)


def couple(row_ref, inverse_ref, coupling_ref):
    width = coupling_ref.shape[2]
    for n in range(inverse_ref.shape[0]):
        coupling_ref[n] = dot_hi(inverse_ref[n], row_ref[n, :, :width])


def leaf_kernel(basis_ref, turned_ref, prior_ref, *refs, top):
    tier = basis_ref.shape[0] - 1
    leaves = 2 ** (tier - top)
    slot_refs, refs = refs[:leaves], refs[leaves:]
    inverse_ref, coupling_ref, row_ref = refs[:3]
    lower_refs, rest_ref, panel_ref = refs[3:-2], refs[-2], refs[-1]
    knots = basis_ref.shape[2]
    pairs = [ref[...] for ref in slot_refs]
    prior = diagonal(prior_ref[tier:tier + 1, :])
    own = gram_block(basis_ref, turned_ref, pairs, tier, tier)
    for n in range(leaves):
        inverse_ref[n] = own[n * knots:(n + 1) * knots] + prior

    def gram(target_ref, pairs, below, other):
        block = gram_block(basis_ref, turned_ref, pairs, below, other)
        columns = slice(other * knots, (other + 1) * knots)
        for n in range(len(pairs)):
            target_ref[n, :, columns] = block[n * knots:(n + 1) * knots]

    others = [functools.partial(gram, row_ref, pairs, tier, other) for other in range(tier)]
    targets = list(lower_refs) + [rest_ref.at[pl.ds(below, 1)] for below in range(top - 1, -1, -1)]
    for target_ref, below in zip(targets, range(tier - 1, -1, -1)):
        if len(pairs) > 1:
            pairs = [pairs[2 * n] + pairs[2 * n + 1] for n in range(len(pairs) // 2)]
        others += [
            functools.partial(gram, target_ref, pairs, below, other) for other in range(below + 1)
        ]
    for below in range(top - 1):
        rest_ref[below, :, (below + 1) * knots:] = jnp.zeros((knots, (top - 1 - below) * knots), f32)
    invert(
        [inverse_ref.at[n] for n in range(leaves)], [panel_ref.at[n] for n in range(leaves)], others
    )
    couple(row_ref, inverse_ref, coupling_ref)
    update(targets[0], tier - 1, row_ref, coupling_ref)


def inner_kernel(*refs, top, count):
    row_ref, coupling_ref = refs[:2]
    row_refs, (rest_in, prior_ref), refs = refs[2:2 + count], refs[2 + count:4 + count], refs[4 + count:]
    inverse_refs, coupling_refs, refs = refs[:count], refs[count:2 * count], refs[2 * count:]
    rest_ref, panel_ref, work_refs = refs[0], refs[1], refs[2:]
    knots = prior_ref.shape[1]
    for work_ref, ref in zip(work_refs, row_refs):
        work_ref[...] = ref[...]
    rest_ref[...] = rest_in[...]
    targets = list(work_refs) + [rest_ref.at[pl.ds(below, 1)] for below in range(top - 1, -1, -1)]
    for i in range(count):
        tier = top + count - 1 - i
        nodes = work_refs[i].shape[0]
        prior = diagonal(prior_ref[tier:tier + 1, :])
        for n in range(nodes):
            inverse_refs[i][n] = work_refs[i][n, :, tier * knots:] + prior
        others = [
            functools.partial(update, targets[i + tier - below], below, row_ref, coupling_ref)
            for below in range(tier - 1, -1, -1)
        ]
        invert(
            [inverse_refs[i].at[n] for n in range(nodes)],
            [panel_ref.at[n] for n in range(nodes)],
            others,
        )
        couple(work_refs[i], inverse_refs[i], coupling_refs[i])
        row_ref, coupling_ref = work_refs[i], coupling_refs[i]
        if i + 1 < count:
            update(targets[i + 1], tier - 1, row_ref, coupling_ref)
    for below in range(top - 1, -1, -1):
        update(targets[count + top - 1 - below], below, row_ref, coupling_ref)


def whole_call(kernel, args, shapes, scratch, name, limit=8, flops=10**10):
    return pl.pallas_call(
        kernel,
        in_specs=[vmem] * len(args),
        out_specs=[vmem] * len(shapes),
        out_shape=[jax.ShapeDtypeStruct(shape, f32) for shape in shapes],
        scratch_shapes=[pltpu.VMEM(shape, f32) for shape in scratch],
        compiler_params=pltpu.CompilerParams(vmem_limit_bytes=limit * 2**20),
        cost_estimate=pl.CostEstimate(flops=flops, bytes_accessed=2**20, transcendentals=0),
        name=name,
    )(*args)


def leaf_tier(slots, basis_table, turned, prior_precision, top):
    tier_count, _, knots = basis_table.shape
    tier = tier_count - 1
    leaves = len(slots)
    shapes = [(leaves, knots, knots)] + [(leaves, knots, tier * knots)] * 2
    shapes += [(2 ** (t - top), knots, (t + 1) * knots) for t in range(tier - 1, top - 1, -1)]
    shapes.append((top, knots, top * knots))
    inverse, coupling, row, *lower, rest = whole_call(
        functools.partial(leaf_kernel, top=top),
        (basis_table, turned, prior_precision, *slots),
        shapes, [(leaves, knots, knots)], "leaf_tier", limit=16, flops=2 * 10**10,
    )
    return inverse, coupling, row, lower, rest


def inner_tiers(row, coupling, lower, rest, prior_precision, top):
    knots = prior_precision.shape[1]
    count = len(lower)
    nodes = [value.shape[0] for value in lower]
    shapes = [(n, knots, knots) for n in nodes]
    shapes += [(n, knots, value.shape[2] - knots) for n, value in zip(nodes, lower)]
    shapes.append(rest.shape)
    out = whole_call(
        functools.partial(inner_kernel, top=top, count=count),
        (row, coupling, *lower, rest, prior_precision),
        shapes, [(max(nodes), knots, knots)] + [value.shape for value in lower],
        "inner_tiers", limit=16, flops=2 * 10**10,
    )
    rest = out[-1].reshape(top * knots, top * knots)
    return list(out[:count]), list(out[count:-1]), rest


def forward_kernel(*refs, leaves):
    slot_refs, refs = refs[:leaves], refs[leaves:]
    out_refs = refs[-2:]
    coupling_refs = refs[:-2]
    knots = coupling_refs[0].shape[1]
    current = [ref[...] for ref in slot_refs]
    own = []
    for ref in coupling_refs:
        width = ref.shape[2]
        own.append(current[0][:, width:width + knots])
        reduced = [
            c[:, :width] - dot_hi(c[:, width:width + knots], ref[n]) for n, c in enumerate(current)
        ]
        current = (
            [reduced[2 * n] + reduced[2 * n + 1] for n in range(len(reduced) // 2)]
            if len(reduced) > 1 else reduced
        )
    out_refs[0][...] = current[0]
    out_refs[1][...] = jnp.concatenate(own, axis=1)


def forward(slots, couplings):
    fields = slots[0].shape[0]
    knots, width = couplings[-1].shape[1:]
    return pl.pallas_call(
        functools.partial(forward_kernel, leaves=len(slots)),
        in_specs=[vmem] * (len(slots) + len(couplings)),
        out_specs=[vmem] * 2,
        out_shape=[
            jax.ShapeDtypeStruct((fields, width), f32),
            jax.ShapeDtypeStruct((fields, knots * len(couplings)), f32),
        ],
        compiler_params=pltpu.CompilerParams(vmem_limit_bytes=8 * 2**20),
        name="forward",
    )(*slots, *couplings)


def top_step(total, prior_row, inverse_ref, panel_ref):
    knots = inverse_ref.shape[0]
    row = total[knots:]
    inverse_ref[...] = row[:, knots:] + diagonal(prior_row)
    invert([inverse_ref], [panel_ref])
    coupling = dot_hi(inverse_ref[...], row[:, :knots])
    return coupling, total[:knots, :knots] - dot_tn(row[:, :knots], coupling)


def root_step(schur, prior_row, inverse_ref, panel_ref):
    inverse_ref[...] = schur + diagonal(prior_row)
    invert([inverse_ref], [panel_ref])


def both_kernel(rest_ref, other_ref, prior_ref, top_ref, coupling_ref, root_ref, panel_ref):
    coupling_ref[...], schur = top_step(
        rest_ref[...] + other_ref[...], prior_ref[1:2, :], top_ref, panel_ref
    )
    root_step(schur, prior_ref[0:1, :], root_ref, panel_ref)


def top_kernel(rest_ref, other_ref, prior_ref, top_ref, coupling_ref, schur_ref, panel_ref):
    coupling_ref[...], schur_ref[...] = top_step(
        rest_ref[...] + other_ref[...], prior_ref[1:2, :], top_ref, panel_ref
    )


def root_kernel(schur_ref, prior_ref, root_ref, panel_ref):
    root_step(schur_ref[...], prior_ref[0:1, :], root_ref, panel_ref)


def right_kernel(right_ref, other_ref, coupling_ref, out_ref):
    knots = coupling_ref.shape[0]
    right = right_ref[...] + other_ref[...]
    out_ref[:, knots:] = right[:, knots:]
    out_ref[:, :knots] = right[:, :knots] - dot_hi(right[:, knots:], coupling_ref[...])


def path_step(path, right, inverse, coupling):
    local = dot_hi(right, inverse) - dot_nt(path, coupling, highest)
    return jnp.concatenate([path, local], axis=1)


def descend_kernel(right_ref, other_ref, top_ref, coupling_ref, root_ref, own_ref, *refs, reduced):
    refs, out_ref = refs[:-1], refs[-1]
    count = len(refs) // 2
    knots = top_ref.shape[0]
    right = right_ref[...]
    if reduced:
        root_right = right[:, :knots]
    else:
        right = right + other_ref[...]
        root_right = right[:, :knots] - dot_hi(right[:, knots:], coupling_ref[...])
    path = dot_hi(root_right, root_ref[...])
    path = path_step(path, right[:, knots:], top_ref[...], coupling_ref[...])
    for depth in range(count - 1, -1, -1):
        own = own_ref[:, depth * knots:(depth + 1) * knots]
        path = path_step(path, own, refs[depth][0], refs[count + depth][0])
    out_ref[...] = path


def path_weights(rest, right, own, prior_precision, inverses, couplings, leaves):
    knots = prior_precision.shape[1]
    fields = right.shape[0]
    square = (knots, knots)
    region_count = lax.axis_size("region")
    other_right = moved(right, leaves, (leaves // 2, 1), (leaves // 2, 1))
    ends = (rest, swapped(rest, "obs", 1), prior_precision)
    reduced = region_count > leaves
    if reduced:
        top, coupling, schur = whole_call(top_kernel, ends, [square] * 3, [square], "top")
        schur = sum_over(schur, "region", leaves, region_count)
        root = whole_call(root_kernel, (schur, prior_precision), [square], [square], "root")[0]
        right = whole_call(right_kernel, (right, other_right, coupling), [right.shape], [], "right")[0]
        other_right = sum_over(right[:, :knots], "region", leaves, region_count)
        right = jnp.concatenate([other_right, right[:, knots:]], axis=1)
    else:
        top, coupling, root = whole_call(both_kernel, ends, [square] * 3, [square], "top_and_root")
    args = (right, other_right, top, coupling, root, own, *inverses, *couplings)
    shape = (fields, prior_precision.shape[0] * knots)
    kernel = functools.partial(descend_kernel, reduced=reduced)
    return whole_call(kernel, args, [shape], [], "descend", flops=10**9)[0]


def fitted_kernel(pattern_ref, amplitude_ref, weight_ref, turned_ref, out_ref, table):
    tier_count, knots, pattern_count = turned_ref.shape
    field_count = weight_ref.shape[0]

    @pl.when(pl.program_id(0) == 0)
    def _():
        for tier in range(tier_count):
            high, low = split(weight_ref[:, tier * knots:(tier + 1) * knots])
            table[tier * field_count:(tier + 1) * field_count, :] = (
                dot(high, turned_ref[tier]) + dot(low, turned_ref[tier])
            ).astype(bf16)

    picked = dot(table[...], one_hot(pattern_ref[...], pattern_count))
    amp = amplitude_ref[...]
    total = picked[:field_count] * amp[0:1]
    for tier in range(1, tier_count):
        total = total + picked[tier * field_count:(tier + 1) * field_count] * amp[tier:tier + 1]
    out_ref[...] = total


def fitted_fields(pattern, amplitude, weights, turned):
    tier_count, knots, pattern_count = turned.shape
    obs = pattern.shape[0]
    field_count = weights.shape[0]
    block = min(2048, obs)
    return pl.pallas_call(
        fitted_kernel,
        grid=(obs // block,),
        in_specs=[
            pl.BlockSpec((1, block), lambda i: (0, i)),
            pl.BlockSpec((tier_count, block), lambda i: (0, i)),
            pl.BlockSpec(weights.shape, lambda i: (0, 0)),
            pl.BlockSpec(turned.shape, lambda i: (0, 0, 0)),
        ],
        out_specs=pl.BlockSpec((field_count, block), lambda i: (0, i)),
        out_shape=jax.ShapeDtypeStruct((field_count, obs), f32),
        scratch_shapes=[pltpu.VMEM((tier_count * field_count, pattern_count), bf16)],
        compiler_params=pltpu.CompilerParams(vmem_limit_bytes=16 * 2**20),
        name="fitted_fields",
    )(pattern.reshape(1, obs), amplitude, weights, turned)


def swapped(value, axis, mask):
    pairs = [(source, source ^ mask) for source in range(lax.axis_size(axis))]
    return lax.ppermute(value, axis, pairs)


def sum_over(value, axis, first_mask, size):
    mask = first_mask
    while mask < size:
        value = value + swapped(value, axis, mask)
        mask *= 2
    return value


def in_own_half(leaves):
    return (lax.axis_index("region") % leaves) // (leaves // 2) == lax.axis_index("obs") % 2


def moved(value, leaves, own_move, other_move):
    region_count, obs_count = lax.axis_size("region"), lax.axis_size("obs")
    pairs = []
    for region in range(region_count):
        for obs in range(obs_count):
            own = (region % leaves) // (leaves // 2) == obs % 2
            region_mask, obs_mask = own_move if own else other_move
            target = (region ^ region_mask) * obs_count + (obs ^ obs_mask)
            pairs.append((region * obs_count + obs, target))
    return lax.ppermute(value, ("region", "obs"), pairs)


def sum_for_half(value, leaves):
    half = leaves // 2
    parts = lax.axis_size("obs") // 2
    got = [
        moved(value, leaves, (0, 2 * max(offset, 1)), (half, 1 ^ 2 * offset))
        for offset in range(parts)
    ]
    own = value
    for part in got[1:]:
        own = own + part
    other = got[0]
    for part in got[1:]:
        other = other + part
    return jnp.where(in_own_half(leaves), own, other)


def gather_half(value, leaves):
    return [value] + [swapped(value, "region", offset) for offset in range(1, leaves // 2)]


def spread_weights(weights, leaves):
    return jnp.where(in_own_half(leaves), weights, swapped(weights, "obs", 1))


def shards(pattern, amplitude, basis_table, fields, prior_precision):
    tier_count = basis_table.shape[0]
    leaves = 2 ** (tier_count - 2)
    order = tier_count * basis_table.shape[2]
    turned = jnp.swapaxes(basis_table, 1, 2)
    sums = statistics(pattern, amplitude, fields, basis_table)
    pair_rows = sums.shape[0] - fields.shape[0]
    sums = sums + swapped(sums, "obs", 1)
    pairs, project = sums[:pair_rows, :basis_table.shape[1]], sums[pair_rows:, :order]
    pairs = sum_for_half(pairs, leaves)
    pair_slots = gather_half(pairs, leaves)
    pair_slots, project = lax.optimization_barrier((pair_slots, project))
    inverse, coupling, row, lower, rest = leaf_tier(
        pair_slots, basis_table, turned, prior_precision, 2
    )
    project = sum_over(project, "obs", 2, lax.axis_size("obs"))
    lower, rest, project = lax.optimization_barrier((lower, rest, project))
    inverses, couplings, rest = inner_tiers(row, coupling, lower, rest, prior_precision, 2)
    inverses, couplings = [inverse] + inverses, [coupling] + couplings
    project_slots = gather_half(project, leaves)
    right, own = forward(project_slots, couplings)
    rest, right = lax.optimization_barrier((rest, right))
    weights = path_weights(rest, right, own, prior_precision, inverses, couplings, leaves)
    weights = spread_weights(weights, leaves)
    return fitted_fields(pattern, amplitude, weights, turned)


def solution(mesh):
    return jax.shard_map(
        shards,
        mesh=mesh,
        in_specs=(
            P(("region", "obs")),
            P(None, ("region", "obs")),
            P(),
            P(None, ("region", "obs")),
            P(),
        ),
        out_specs=P(None, ("region", "obs")),
        check_vma=False,
    )
```

```python
import functools

import jax
import jax.numpy as jnp
from jax import lax
from jax.experimental import pallas as pl
from jax.experimental.pallas import tpu as pltpu
from jax.sharding import PartitionSpec as P

highest = lax.Precision.HIGHEST
f32 = jnp.float32
bf16 = jnp.bfloat16
SUB = 8
vmem = pl.BlockSpec(memory_space=pltpu.VMEM)
PANELS = {1: (64, 2), 2: (32, 2)}


def pair_index(tier, other):
    return tier * (tier + 1) // 2 + other


def dot(a, b):
    return jnp.dot(a, b, preferred_element_type=f32)


def dot_nt(a, b, precision=None):
    return lax.dot_general(
        a, b, (((1,), (1,)), ((), ())), precision=precision, preferred_element_type=f32
    )


def dot_tn(a, b):
    return lax.dot_general(
        a, b, (((0,), (0,)), ((), ())), precision=highest, preferred_element_type=f32
    )


def dot_hi(a, b):
    return jnp.dot(a, b, precision=highest, preferred_element_type=f32)


def split(value):
    high = value.astype(bf16)
    return high, (value - high.astype(f32)).astype(bf16)


def split3(value):
    high = value.astype(bf16)
    rest = value - high.astype(f32)
    middle = rest.astype(bf16)
    return high, middle, (rest - middle.astype(f32)).astype(bf16)


def one_hot(pattern_row, pattern_count):
    rows = lax.broadcasted_iota(jnp.int16, (pattern_count, pattern_row.shape[1]), 0)
    return jnp.where(rows == pattern_row.astype(jnp.int16), jnp.asarray(1, bf16), jnp.asarray(0, bf16))


def stats_kernel(pattern_ref, amplitude_ref, fields_ref, basis_ref, out_ref, prods, acc):
    step = pl.program_id(0)
    tier_count, pattern_count, knots = basis_ref.shape
    field_count = fields_ref.shape[0]
    pair_rows = prods.shape[0]
    amp = amplitude_ref[...]
    prods[...] = jnp.zeros_like(prods)
    for tier in range(tier_count):
        first = pair_index(tier, 0)
        prods[first:first + tier + 1, :] = amp[:tier + 1] * amp[tier:tier + 1]
    pair_parts = split3(prods[...])
    plain = fields_ref[...]
    field_rows = plain.astype(f32)
    shifted = amp - 1.0
    values = jnp.concatenate(
        [*pair_parts, plain]
        + [(field_rows * shifted[tier:tier + 1]).astype(bf16) for tier in range(tier_count)],
        axis=0,
    )
    part = dot_nt(values, one_hot(pattern_ref[...], pattern_count))

    @pl.when(step == 0)
    def _():
        acc[...] = part

    @pl.when(step > 0)
    def _():
        acc[...] += part

    @pl.when(step == pl.num_programs(0) - 1)
    def _():
        base = 3 * pair_rows
        out_ref[...] = jnp.zeros_like(out_ref)
        out_ref[:pair_rows, :pattern_count] = acc[:pair_rows] + (
            acc[pair_rows:2 * pair_rows] + acc[2 * pair_rows:base]
        )
        plain_sum = acc[base:base + field_count]
        for tier in range(tier_count):
            first = base + (tier + 1) * field_count
            high, low = split(plain_sum + acc[first:first + field_count])
            out_ref[pair_rows:, tier * knots:(tier + 1) * knots] = (
                dot(high, basis_ref[tier]) + dot(low, basis_ref[tier])
            )


def statistics(pattern, amplitude, fields, basis_table):
    tier_count, pattern_count, knots = basis_table.shape
    field_count, obs = fields.shape
    block = min(8192, obs)
    pair_rows = -(-pair_index(tier_count, 0) // 16) * 16
    rows = 3 * pair_rows + (1 + tier_count) * field_count
    width = max(pattern_count, tier_count * knots)
    return pl.pallas_call(
        stats_kernel,
        grid=(obs // block,),
        in_specs=[
            pl.BlockSpec((1, block), lambda i: (0, i)),
            pl.BlockSpec((tier_count, block), lambda i: (0, i)),
            pl.BlockSpec((field_count, block), lambda i: (0, i)),
            pl.BlockSpec(basis_table.shape, lambda i: (0, 0, 0)),
        ],
        out_specs=pl.BlockSpec((pair_rows + field_count, width), lambda i: (0, 0)),
        out_shape=pltpu.VMEM((pair_rows + field_count, width), f32),
        scratch_shapes=[
            pltpu.VMEM((pair_rows, block), f32),
            pltpu.VMEM((rows, pattern_count), f32),
        ],
        compiler_params=pltpu.CompilerParams(vmem_limit_bytes=58 * 2**20),
        cost_estimate=pl.CostEstimate(
            flops=2 * rows * pattern_count * obs, bytes_accessed=4 * 2**20, transcendentals=0
        ),
        name="statistics",
    )(pattern.reshape(1, obs), amplitude, fields, basis_table)


def along_rows(x, row):
    return jnp.broadcast_to(x[row:row + 1, :], x.shape)


def along_lanes(x, lane):
    return jnp.broadcast_to(x[:, lane:lane + 1], x.shape)


def tree_sum(values):
    while len(values) > 1:
        ends = values[len(values) - len(values) % 2:]
        values = [values[i] + values[i + 1] for i in range(0, len(values) - 1, 2)] + ends
    return values[0]


def sweep(rows, first, group, lane0, sub, lane):
    count, blocks, size = len(rows), len(rows[0]), SUB * group
    here = (lane >= lane0) & (lane < lane0 + size)
    columns, pivot = [], []
    for m in range(count):
        block = rows[m][first:first + group]
        columns.append([[along_lanes(b, lane0 + j) for b in block] for j in range(size)])
        pivot.append([
            jnp.where(here, (lane - lane0 - SUB * a == sub).astype(f32), b)
            for a, b in enumerate(block)
        ])
    for k in range(size):
        at, row = divmod(k, SUB)
        is_row = sub == row
        scale = [
            pltpu.reciprocal(along_rows(columns[m][k][at], row), approx=True) for m in range(count)
        ]

        def eliminated(parts, m):
            scaled = along_rows(parts[at], row) * scale[m]
            out = [part - c * scaled for part, c in zip(parts, columns[m][k])]
            out[at] = jnp.where(is_row, scaled, out[at])
            return out

        for j in range(k + 1, size):
            for m in range(count):
                columns[m][j] = eliminated(columns[m][j], m)
        for m in range(count):
            pivot[m] = eliminated(pivot[m], m)
    solved = [[along_rows(pivot[m][j // SUB], j % SUB) for j in range(size)] for m in range(count)]
    out = [list(r) for r in rows]
    for step in range(blocks - group):
        i = (first + group + step) % blocks
        for m in range(count):
            total = tree_sum([along_lanes(rows[m][i], lane0 + j) * solved[m][j] for j in range(size)])
            out[m][i] = jnp.where(here, 0.0, rows[m][i]) - total
    for m in range(count):
        out[m][first:first + group] = pivot[m]
    return out


def invert(refs, panel_refs, others=()):
    others = list(others)
    size = refs[0].shape[0]
    count = len(refs)
    panel, group = PANELS.get(count, (16, 1))
    panel = min(panel, size)
    blocks = panel // SUB
    steps = size // (SUB * group)
    each = -(-len(others) // steps)
    sub = lax.broadcasted_iota(jnp.int32, (SUB, size), 0)
    lane = lax.broadcasted_iota(jnp.int32, (SUB, size), 1)
    wide = lax.broadcasted_iota(jnp.int32, (size, size), 1)
    for m in range(count):
        panel_refs[m][...] = jnp.zeros((size, size), f32)
    for p in range(size // panel):
        first = p * panel
        rows = [
            [refs[m][first + SUB * i:first + SUB * (i + 1), :] for i in range(blocks)]
            for m in range(count)
        ]
        for q in range(0, blocks, group):
            for work in others[:each]:
                work()
            others = others[each:]
            rows = sweep(rows, q, group, first + SUB * q, sub, lane)
        for m in range(count):
            if p > 0:
                panel_refs[m][first - panel:first, :] = jnp.zeros((panel, size), f32)
            for i in range(blocks):
                panel_refs[m][first + SUB * i:first + SUB * (i + 1), :] = rows[m][i]
        old = [refs[m][...] for m in range(count)]
        change = [dot_hi(old[m], panel_refs[m][...]) for m in range(count)]
        here = (wide >= first) & (wide < first + panel)
        for m in range(count):
            refs[m][...] = jnp.where(here, 0.0, old[m]) - change[m]
            for i in range(blocks):
                refs[m][first + SUB * i:first + SUB * (i + 1), :] = rows[m][i]


def diagonal(row):
    size = row.shape[1]
    rows = lax.broadcasted_iota(jnp.int32, (size, size), 0)
    columns = lax.broadcasted_iota(jnp.int32, (size, size), 1)
    return jnp.where(rows == columns, row, 0.0)


def gram_block(basis_ref, turned_ref, pairs, tier, other):
    turned = turned_ref[tier].astype(f32)
    index = pair_index(tier, other)
    parts = zip(*[split3(turned * pair[index:index + 1, :]) for pair in pairs])
    product = dot(jnp.concatenate(sum(parts, ()), axis=0), basis_ref[other])
    size = len(pairs) * turned.shape[0]
    return product[:size] + (product[size:2 * size] + product[2 * size:])


def update(target_ref, below, row_ref, coupling_ref):
    nodes, knots = row_ref.shape[:2]
    share = nodes // target_ref.shape[0]
    first, last = below * knots, (below + 1) * knots
    for n in range(target_ref.shape[0]):
        part = slice(n * share, (n + 1) * share)
        left = row_ref[part, :, first:last].reshape(share * knots, knots)
        right = coupling_ref[part, :, :last].reshape(share * knots, last)
        target_ref[n, :, :last] -= dot_tn(left, right)


def couple(row_ref, inverse_ref, coupling_ref):
    width = coupling_ref.shape[2]
    for n in range(inverse_ref.shape[0]):
        coupling_ref[n] = dot_hi(inverse_ref[n], row_ref[n, :, :width])


def leaf_kernel(basis_ref, turned_ref, prior_ref, *refs, top):
    tier = basis_ref.shape[0] - 1
    leaves = 2 ** (tier - top)
    slot_refs, refs = refs[:leaves], refs[leaves:]
    inverse_ref, coupling_ref, row_ref = refs[:3]
    lower_refs, rest_ref, panel_ref = refs[3:-2], refs[-2], refs[-1]
    knots = basis_ref.shape[2]
    pairs = [ref[...] for ref in slot_refs]
    prior = diagonal(prior_ref[tier:tier + 1, :])
    own = gram_block(basis_ref, turned_ref, pairs, tier, tier)
    for n in range(leaves):
        inverse_ref[n] = own[n * knots:(n + 1) * knots] + prior

    def gram(target_ref, pairs, below, other):
        block = gram_block(basis_ref, turned_ref, pairs, below, other)
        columns = slice(other * knots, (other + 1) * knots)
        for n in range(len(pairs)):
            target_ref[n, :, columns] = block[n * knots:(n + 1) * knots]

    others = [functools.partial(gram, row_ref, pairs, tier, other) for other in range(tier)]
    targets = list(lower_refs) + [rest_ref.at[pl.ds(below, 1)] for below in range(top - 1, -1, -1)]
    for target_ref, below in zip(targets, range(tier - 1, -1, -1)):
        if len(pairs) > 1:
            pairs = [pairs[2 * n] + pairs[2 * n + 1] for n in range(len(pairs) // 2)]
        others += [
            functools.partial(gram, target_ref, pairs, below, other) for other in range(below + 1)
        ]
    for below in range(top - 1):
        rest_ref[below, :, (below + 1) * knots:] = jnp.zeros((knots, (top - 1 - below) * knots), f32)
    invert(
        [inverse_ref.at[n] for n in range(leaves)], [panel_ref.at[n] for n in range(leaves)], others
    )
    couple(row_ref, inverse_ref, coupling_ref)
    update(targets[0], tier - 1, row_ref, coupling_ref)


def inner_kernel(*refs, top, count):
    row_ref, coupling_ref = refs[:2]
    row_refs, (rest_in, prior_ref), refs = refs[2:2 + count], refs[2 + count:4 + count], refs[4 + count:]
    inverse_refs, coupling_refs, refs = refs[:count], refs[count:2 * count], refs[2 * count:]
    rest_ref, panel_ref, work_refs = refs[0], refs[1], refs[2:]
    knots = prior_ref.shape[1]
    for work_ref, ref in zip(work_refs, row_refs):
        work_ref[...] = ref[...]
    rest_ref[...] = rest_in[...]
    targets = list(work_refs) + [rest_ref.at[pl.ds(below, 1)] for below in range(top - 1, -1, -1)]
    for i in range(count):
        tier = top + count - 1 - i
        nodes = work_refs[i].shape[0]
        prior = diagonal(prior_ref[tier:tier + 1, :])
        for n in range(nodes):
            inverse_refs[i][n] = work_refs[i][n, :, tier * knots:] + prior
        others = [
            functools.partial(update, targets[i + tier - below], below, row_ref, coupling_ref)
            for below in range(tier - 1, -1, -1)
        ]
        invert(
            [inverse_refs[i].at[n] for n in range(nodes)],
            [panel_ref.at[n] for n in range(nodes)],
            others,
        )
        couple(work_refs[i], inverse_refs[i], coupling_refs[i])
        row_ref, coupling_ref = work_refs[i], coupling_refs[i]
        if i + 1 < count:
            update(targets[i + 1], tier - 1, row_ref, coupling_ref)
    for below in range(top - 1, -1, -1):
        update(targets[count + top - 1 - below], below, row_ref, coupling_ref)


def whole_call(kernel, args, shapes, scratch, name, limit=8, flops=10**10):
    return pl.pallas_call(
        kernel,
        in_specs=[vmem] * len(args),
        out_specs=[vmem] * len(shapes),
        out_shape=[jax.ShapeDtypeStruct(shape, f32) for shape in shapes],
        scratch_shapes=[pltpu.VMEM(shape, f32) for shape in scratch],
        compiler_params=pltpu.CompilerParams(vmem_limit_bytes=limit * 2**20),
        cost_estimate=pl.CostEstimate(flops=flops, bytes_accessed=2**20, transcendentals=0),
        name=name,
    )(*args)


def leaf_tier(slots, basis_table, turned, prior_precision, top):
    tier_count, _, knots = basis_table.shape
    tier = tier_count - 1
    leaves = len(slots)
    shapes = [(leaves, knots, knots)] + [(leaves, knots, tier * knots)] * 2
    shapes += [(2 ** (t - top), knots, (t + 1) * knots) for t in range(tier - 1, top - 1, -1)]
    shapes.append((top, knots, top * knots))
    inverse, coupling, row, *lower, rest = whole_call(
        functools.partial(leaf_kernel, top=top),
        (basis_table, turned, prior_precision, *slots),
        shapes, [(leaves, knots, knots)], "leaf_tier", limit=16, flops=2 * 10**10,
    )
    return inverse, coupling, row, lower, rest


def inner_tiers(row, coupling, lower, rest, prior_precision, top):
    knots = prior_precision.shape[1]
    count = len(lower)
    nodes = [value.shape[0] for value in lower]
    shapes = [(n, knots, knots) for n in nodes]
    shapes += [(n, knots, value.shape[2] - knots) for n, value in zip(nodes, lower)]
    shapes.append(rest.shape)
    out = whole_call(
        functools.partial(inner_kernel, top=top, count=count),
        (row, coupling, *lower, rest, prior_precision),
        shapes, [(max(nodes), knots, knots)] + [value.shape for value in lower],
        "inner_tiers", limit=16, flops=2 * 10**10,
    )
    rest = out[-1].reshape(top * knots, top * knots)
    return list(out[:count]), list(out[count:-1]), rest


def forward_kernel(*refs, leaves):
    slot_refs, refs = refs[:leaves], refs[leaves:]
    out_refs = refs[-2:]
    coupling_refs = refs[:-2]
    knots = coupling_refs[0].shape[1]
    current = [ref[...] for ref in slot_refs]
    own = []
    for ref in coupling_refs:
        width = ref.shape[2]
        own.append(current[0][:, width:width + knots])
        reduced = [
            c[:, :width] - dot_hi(c[:, width:width + knots], ref[n]) for n, c in enumerate(current)
        ]
        current = (
            [reduced[2 * n] + reduced[2 * n + 1] for n in range(len(reduced) // 2)]
            if len(reduced) > 1 else reduced
        )
    out_refs[0][...] = current[0]
    out_refs[1][...] = jnp.concatenate(own, axis=1)


def forward(slots, couplings):
    fields = slots[0].shape[0]
    knots, width = couplings[-1].shape[1:]
    return pl.pallas_call(
        functools.partial(forward_kernel, leaves=len(slots)),
        in_specs=[vmem] * (len(slots) + len(couplings)),
        out_specs=[vmem] * 2,
        out_shape=[
            jax.ShapeDtypeStruct((fields, width), f32),
            jax.ShapeDtypeStruct((fields, knots * len(couplings)), f32),
        ],
        compiler_params=pltpu.CompilerParams(vmem_limit_bytes=8 * 2**20),
        name="forward",
    )(*slots, *couplings)


def composites(own_ref, refs, local_ref, deep_ref):
    count = len(refs) // 2
    inverse_refs, coupling_refs = refs[:count], refs[count:]
    knots = inverse_refs[0].shape[1]
    wide = deep_ref.shape[1]

    def solve(depth):
        place = slice((count - 1 - depth) * knots, (count - depth) * knots)
        own = own_ref[:, depth * knots:(depth + 1) * knots]
        local_ref[:, place] = dot_hi(own, inverse_refs[depth][0])

    def shorten(depth):
        first = (count - 1 - depth) * knots
        deep = coupling_refs[depth][0, :, :wide]
        if first > 0:
            between = coupling_refs[depth][0, :, wide:]
            deep = deep - dot_hi(between, deep_ref[:first, :])
            local_ref[:, first:first + knots] -= dot_nt(local_ref[:, :first], between, highest)
        deep_ref[first:first + knots, :] = deep

    depths = range(count - 1, -1, -1)
    return [functools.partial(solve, d) for d in depths] + [
        functools.partial(shorten, d) for d in depths
    ]


def top_step(total, prior_row, inverse_ref, panel_ref, others):
    knots = inverse_ref.shape[0]
    row = total[knots:]
    inverse_ref[...] = row[:, knots:] + diagonal(prior_row)
    invert([inverse_ref], [panel_ref], others)
    coupling = dot_hi(inverse_ref[...], row[:, :knots])
    return coupling, total[:knots, :knots] - dot_tn(row[:, :knots], coupling)


def root_step(schur, prior_row, inverse_ref, panel_ref):
    inverse_ref[...] = schur + diagonal(prior_row)
    invert([inverse_ref], [panel_ref])


def top_kernel(rest_ref, other_ref, prior_ref, own_ref, *refs, both):
    refs, outs = refs[:-6], refs[-6:]
    local_ref, deep_ref, top_ref, coupling_ref, last_ref, panel_ref = outs
    coupling_ref[...], schur = top_step(
        rest_ref[...] + other_ref[...], prior_ref[1:2, :], top_ref, panel_ref,
        composites(own_ref, refs, local_ref, deep_ref),
    )
    if both:
        root_step(schur, prior_ref[0:1, :], last_ref, panel_ref)
    else:
        last_ref[...] = schur


def root_kernel(schur_ref, prior_ref, root_ref, panel_ref):
    root_step(schur_ref[...], prior_ref[0:1, :], root_ref, panel_ref)


def right_kernel(right_ref, other_ref, coupling_ref, out_ref):
    knots = coupling_ref.shape[0]
    right = right_ref[...] + other_ref[...]
    out_ref[:, knots:] = right[:, knots:]
    out_ref[:, :knots] = right[:, :knots] - dot_hi(right[:, knots:], coupling_ref[...])


def descend_kernel(right_ref, other_ref, top_ref, coupling_ref, root_ref, local_ref, deep_ref,
                   out_ref, *, reduced):
    knots = top_ref.shape[0]
    right = right_ref[...]
    if reduced:
        root_right = right[:, :knots]
    else:
        right = right + other_ref[...]
        root_right = right[:, :knots] - dot_hi(right[:, knots:], coupling_ref[...])
    first = dot_hi(root_right, root_ref[...])
    second = dot_hi(right[:, knots:], top_ref[...]) - dot_nt(first, coupling_ref[...], highest)
    tops = jnp.concatenate([first, second], axis=1)
    out_ref[:, :2 * knots] = tops
    out_ref[:, 2 * knots:] = local_ref[...] - dot_nt(tops, deep_ref[...], highest)


def path_weights(rest, right, own, prior_precision, inverses, couplings, leaves):
    knots = prior_precision.shape[1]
    fields = right.shape[0]
    square = (knots, knots)
    region_count = lax.axis_size("region")
    other_right = moved(right, leaves, (leaves // 2, 1), (leaves // 2, 1))
    reduced = region_count > leaves
    args = (rest, swapped(rest, "obs", 1), prior_precision, own, *inverses, *couplings)
    shapes = [(fields, own.shape[1]), (own.shape[1], 2 * knots), square, square, square]
    local, deep, top, coupling, root = whole_call(
        functools.partial(top_kernel, both=not reduced), args, shapes, [square], "top"
    )
    if reduced:
        schur = sum_over(root, "region", leaves, region_count)
        root = whole_call(root_kernel, (schur, prior_precision), [square], [square], "root")[0]
        right = whole_call(right_kernel, (right, other_right, coupling), [right.shape], [], "right")[0]
        other_right = sum_over(right[:, :knots], "region", leaves, region_count)
        right = jnp.concatenate([other_right, right[:, knots:]], axis=1)
    args = (right, other_right, top, coupling, root, local, deep)
    shape = (fields, prior_precision.shape[0] * knots)
    kernel = functools.partial(descend_kernel, reduced=reduced)
    return whole_call(kernel, args, [shape], [], "descend", flops=10**9)[0]


def fitted_kernel(pattern_ref, amplitude_ref, weight_ref, turned_ref, out_ref, table):
    tier_count, knots, pattern_count = turned_ref.shape
    field_count = weight_ref.shape[0]

    @pl.when(pl.program_id(0) == 0)
    def _():
        for tier in range(tier_count):
            high, low = split(weight_ref[:, tier * knots:(tier + 1) * knots])
            table[tier * field_count:(tier + 1) * field_count, :] = (
                dot(high, turned_ref[tier]) + dot(low, turned_ref[tier])
            ).astype(bf16)

    picked = dot(table[...], one_hot(pattern_ref[...], pattern_count))
    amp = amplitude_ref[...]
    total = picked[:field_count] * amp[0:1]
    for tier in range(1, tier_count):
        total = total + picked[tier * field_count:(tier + 1) * field_count] * amp[tier:tier + 1]
    out_ref[...] = total


def fitted_fields(pattern, amplitude, weights, turned):
    tier_count, knots, pattern_count = turned.shape
    obs = pattern.shape[0]
    field_count = weights.shape[0]
    block = min(4096, obs)
    return pl.pallas_call(
        fitted_kernel,
        grid=(obs // block,),
        in_specs=[
            pl.BlockSpec((1, block), lambda i: (0, i)),
            pl.BlockSpec((tier_count, block), lambda i: (0, i)),
            pl.BlockSpec(weights.shape, lambda i: (0, 0)),
            pl.BlockSpec(turned.shape, lambda i: (0, 0, 0)),
        ],
        out_specs=pl.BlockSpec((field_count, block), lambda i: (0, i)),
        out_shape=jax.ShapeDtypeStruct((field_count, obs), f32),
        scratch_shapes=[pltpu.VMEM((tier_count * field_count, pattern_count), bf16)],
        compiler_params=pltpu.CompilerParams(vmem_limit_bytes=16 * 2**20),
        name="fitted_fields",
    )(pattern.reshape(1, obs), amplitude, weights, turned)


def swapped(value, axis, mask):
    pairs = [(source, source ^ mask) for source in range(lax.axis_size(axis))]
    return lax.ppermute(value, axis, pairs)


def sum_over(value, axis, first_mask, size):
    mask = first_mask
    while mask < size:
        value = value + swapped(value, axis, mask)
        mask *= 2
    return value


def in_own_half(leaves):
    return (lax.axis_index("region") % leaves) // (leaves // 2) == lax.axis_index("obs") % 2


def moved(value, leaves, own_move, other_move):
    region_count, obs_count = lax.axis_size("region"), lax.axis_size("obs")
    pairs = []
    for region in range(region_count):
        for obs in range(obs_count):
            own = (region % leaves) // (leaves // 2) == obs % 2
            region_mask, obs_mask = own_move if own else other_move
            target = (region ^ region_mask) * obs_count + (obs ^ obs_mask)
            pairs.append((region * obs_count + obs, target))
    return lax.ppermute(value, ("region", "obs"), pairs)


def sum_for_half(value, leaves):
    half = leaves // 2
    parts = lax.axis_size("obs") // 2
    got = [
        moved(value, leaves, (0, 2 * max(offset, 1)), (half, 1 ^ 2 * offset))
        for offset in range(parts)
    ]
    own = value
    for part in got[1:]:
        own = own + part
    other = got[0]
    for part in got[1:]:
        other = other + part
    return jnp.where(in_own_half(leaves), own, other)


def gather_half(value, leaves):
    return [value] + [swapped(value, "region", offset) for offset in range(1, leaves // 2)]


def spread_weights(weights, leaves):
    return jnp.where(in_own_half(leaves), weights, swapped(weights, "obs", 1))


def shards(pattern, amplitude, basis_table, fields, prior_precision):
    tier_count = basis_table.shape[0]
    leaves = 2 ** (tier_count - 2)
    order = tier_count * basis_table.shape[2]
    turned = jnp.swapaxes(basis_table, 1, 2)
    sums = statistics(pattern, amplitude, fields, basis_table)
    pair_rows = sums.shape[0] - fields.shape[0]
    sums = sums + swapped(sums, "obs", 1)
    pairs, project = sums[:pair_rows, :basis_table.shape[1]], sums[pair_rows:, :order]
    pairs = sum_for_half(pairs, leaves)
    pair_slots = gather_half(pairs, leaves)
    pair_slots, project = lax.optimization_barrier((pair_slots, project))
    inverse, coupling, row, lower, rest = leaf_tier(
        pair_slots, basis_table, turned, prior_precision, 2
    )
    project = sum_over(project, "obs", 2, lax.axis_size("obs"))
    lower, rest, project = lax.optimization_barrier((lower, rest, project))
    inverses, couplings, rest = inner_tiers(row, coupling, lower, rest, prior_precision, 2)
    inverses, couplings = [inverse] + inverses, [coupling] + couplings
    project_slots = gather_half(project, leaves)
    right, own = forward(project_slots, couplings)
    rest, right = lax.optimization_barrier((rest, right))
    weights = path_weights(rest, right, own, prior_precision, inverses, couplings, leaves)
    weights = spread_weights(weights, leaves)
    return fitted_fields(pattern, amplitude, weights, turned)


def solution(mesh):
    return jax.shard_map(
        shards,
        mesh=mesh,
        in_specs=(
            P(("region", "obs")),
            P(None, ("region", "obs")),
            P(),
            P(None, ("region", "obs")),
            P(),
        ),
        out_specs=P(None, ("region", "obs")),
        check_vma=False,
    )
```

```python
import functools

import jax
import jax.numpy as jnp
from jax import lax
from jax.experimental import pallas as pl
from jax.experimental.pallas import tpu as pltpu
from jax.sharding import PartitionSpec as P

highest = lax.Precision.HIGHEST
f32 = jnp.float32
bf16 = jnp.bfloat16
SUB = 8
vmem = pl.BlockSpec(memory_space=pltpu.VMEM)
PANELS = {1: (64, 2), 2: (32, 2)}


def pair_index(tier, other):
    return tier * (tier + 1) // 2 + other


def dot(a, b):
    return jnp.dot(a, b, preferred_element_type=f32)


def dot_nt(a, b, precision=None):
    return lax.dot_general(
        a, b, (((1,), (1,)), ((), ())), precision=precision, preferred_element_type=f32
    )


def dot_tn(a, b):
    return lax.dot_general(
        a, b, (((0,), (0,)), ((), ())), precision=highest, preferred_element_type=f32
    )


def dot_hi(a, b):
    return jnp.dot(a, b, precision=highest, preferred_element_type=f32)


def split(value):
    high = value.astype(bf16)
    return high, (value - high.astype(f32)).astype(bf16)


def split3(value):
    high = value.astype(bf16)
    rest = value - high.astype(f32)
    middle = rest.astype(bf16)
    return high, middle, (rest - middle.astype(f32)).astype(bf16)


def one_hot(pattern_row, pattern_count):
    rows = lax.broadcasted_iota(jnp.int16, (pattern_count, pattern_row.shape[1]), 0)
    return jnp.where(rows == pattern_row.astype(jnp.int16), jnp.asarray(1, bf16), jnp.asarray(0, bf16))


def stats_kernel(pattern_ref, amplitude_ref, fields_ref, basis_ref, out_ref, prods, acc):
    step = pl.program_id(0)
    tier_count, pattern_count, knots = basis_ref.shape
    field_count = fields_ref.shape[0]
    pair_rows = prods.shape[0]
    amp = amplitude_ref[...]
    prods[...] = jnp.zeros_like(prods)
    for tier in range(tier_count):
        first = pair_index(tier, 0)
        prods[first:first + tier + 1, :] = amp[:tier + 1] * amp[tier:tier + 1]
    pair_parts = split3(prods[...])
    plain = fields_ref[...]
    field_rows = plain.astype(f32)
    shifted = amp - 1.0
    values = jnp.concatenate(
        [*pair_parts, plain]
        + [(field_rows * shifted[tier:tier + 1]).astype(bf16) for tier in range(tier_count)],
        axis=0,
    )
    part = dot_nt(values, one_hot(pattern_ref[...], pattern_count))

    @pl.when(step == 0)
    def _():
        acc[...] = part

    @pl.when(step > 0)
    def _():
        acc[...] += part

    @pl.when(step == pl.num_programs(0) - 1)
    def _():
        base = 3 * pair_rows
        out_ref[...] = jnp.zeros_like(out_ref)
        out_ref[:pair_rows, :pattern_count] = acc[:pair_rows] + (
            acc[pair_rows:2 * pair_rows] + acc[2 * pair_rows:base]
        )
        plain_sum = acc[base:base + field_count]
        for tier in range(tier_count):
            first = base + (tier + 1) * field_count
            high, low = split(plain_sum + acc[first:first + field_count])
            out_ref[pair_rows:, tier * knots:(tier + 1) * knots] = (
                dot(high, basis_ref[tier]) + dot(low, basis_ref[tier])
            )


def statistics(pattern, amplitude, fields, basis_table):
    tier_count, pattern_count, knots = basis_table.shape
    field_count, obs = fields.shape
    block = min(8192, obs)
    pair_rows = -(-pair_index(tier_count, 0) // 16) * 16
    rows = 3 * pair_rows + (1 + tier_count) * field_count
    width = max(pattern_count, tier_count * knots)
    return pl.pallas_call(
        stats_kernel,
        grid=(obs // block,),
        in_specs=[
            pl.BlockSpec((1, block), lambda i: (0, i)),
            pl.BlockSpec((tier_count, block), lambda i: (0, i)),
            pl.BlockSpec((field_count, block), lambda i: (0, i)),
            pl.BlockSpec(basis_table.shape, lambda i: (0, 0, 0)),
        ],
        out_specs=pl.BlockSpec((pair_rows + field_count, width), lambda i: (0, 0)),
        out_shape=pltpu.VMEM((pair_rows + field_count, width), f32),
        scratch_shapes=[
            pltpu.VMEM((pair_rows, block), f32),
            pltpu.VMEM((rows, pattern_count), f32),
        ],
        compiler_params=pltpu.CompilerParams(vmem_limit_bytes=58 * 2**20),
        cost_estimate=pl.CostEstimate(
            flops=2 * rows * pattern_count * obs, bytes_accessed=4 * 2**20, transcendentals=0
        ),
        name="statistics",
    )(pattern.reshape(1, obs), amplitude, fields, basis_table)


def along_rows(x, row):
    return jnp.broadcast_to(x[row:row + 1, :], x.shape)


def along_lanes(x, lane):
    return jnp.broadcast_to(x[:, lane:lane + 1], x.shape)


def tree_sum(values):
    while len(values) > 1:
        ends = values[len(values) - len(values) % 2:]
        values = [values[i] + values[i + 1] for i in range(0, len(values) - 1, 2)] + ends
    return values[0]


def sweep(rows, first, group, lane0, sub, lane):
    count, blocks, size = len(rows), len(rows[0]), SUB * group
    here = (lane >= lane0) & (lane < lane0 + size)
    columns, pivot = [], []
    for m in range(count):
        block = rows[m][first:first + group]
        columns.append([[along_lanes(b, lane0 + j) for b in block] for j in range(size)])
        pivot.append([
            jnp.where(here, (lane - lane0 - SUB * a == sub).astype(f32), b)
            for a, b in enumerate(block)
        ])
    for k in range(size):
        at, row = divmod(k, SUB)
        is_row = sub == row
        scale = [
            pltpu.reciprocal(along_rows(columns[m][k][at], row), approx=True) for m in range(count)
        ]

        def eliminated(parts, m):
            scaled = along_rows(parts[at], row) * scale[m]
            out = [part - c * scaled for part, c in zip(parts, columns[m][k])]
            out[at] = jnp.where(is_row, scaled, out[at])
            return out

        for j in range(k + 1, size):
            for m in range(count):
                columns[m][j] = eliminated(columns[m][j], m)
        for m in range(count):
            pivot[m] = eliminated(pivot[m], m)
    solved = [[along_rows(pivot[m][j // SUB], j % SUB) for j in range(size)] for m in range(count)]
    out = [list(r) for r in rows]
    for step in range(blocks - group):
        i = (first + group + step) % blocks
        for m in range(count):
            total = tree_sum([along_lanes(rows[m][i], lane0 + j) * solved[m][j] for j in range(size)])
            out[m][i] = jnp.where(here, 0.0, rows[m][i]) - total
    for m in range(count):
        out[m][first:first + group] = pivot[m]
    return out


def invert(refs, panel_refs, others=()):
    others = list(others)
    size = refs[0].shape[0]
    count = len(refs)
    panel, group = PANELS.get(count, (16, 1))
    panel = min(panel, size)
    blocks = panel // SUB
    steps = size // (SUB * group)
    each = -(-len(others) // steps)
    sub = lax.broadcasted_iota(jnp.int32, (SUB, size), 0)
    lane = lax.broadcasted_iota(jnp.int32, (SUB, size), 1)
    wide = lax.broadcasted_iota(jnp.int32, (size, size), 1)
    for m in range(count):
        panel_refs[m][...] = jnp.zeros((size, size), f32)
    for p in range(size // panel):
        first = p * panel
        rows = [
            [refs[m][first + SUB * i:first + SUB * (i + 1), :] for i in range(blocks)]
            for m in range(count)
        ]
        for q in range(0, blocks, group):
            for work in others[:each]:
                work()
            others = others[each:]
            rows = sweep(rows, q, group, first + SUB * q, sub, lane)
        for m in range(count):
            if p > 0:
                panel_refs[m][first - panel:first, :] = jnp.zeros((panel, size), f32)
            for i in range(blocks):
                panel_refs[m][first + SUB * i:first + SUB * (i + 1), :] = rows[m][i]
        old = [refs[m][...] for m in range(count)]
        change = [dot_hi(old[m], panel_refs[m][...]) for m in range(count)]
        here = (wide >= first) & (wide < first + panel)
        for m in range(count):
            refs[m][...] = jnp.where(here, 0.0, old[m]) - change[m]
            for i in range(blocks):
                refs[m][first + SUB * i:first + SUB * (i + 1), :] = rows[m][i]


def diagonal(row):
    size = row.shape[1]
    rows = lax.broadcasted_iota(jnp.int32, (size, size), 0)
    columns = lax.broadcasted_iota(jnp.int32, (size, size), 1)
    return jnp.where(rows == columns, row, 0.0)


def gram_block(basis_ref, turned_ref, pairs, tier, other):
    turned = turned_ref[tier].astype(f32)
    index = pair_index(tier, other)
    parts = zip(*[split3(turned * pair[index:index + 1, :]) for pair in pairs])
    product = dot(jnp.concatenate(sum(parts, ()), axis=0), basis_ref[other])
    size = len(pairs) * turned.shape[0]
    return product[:size] + (product[size:2 * size] + product[2 * size:])


def update(target_ref, below, row_ref, coupling_ref):
    nodes, knots = row_ref.shape[:2]
    share = nodes // target_ref.shape[0]
    first, last = below * knots, (below + 1) * knots
    for n in range(target_ref.shape[0]):
        part = slice(n * share, (n + 1) * share)
        left = row_ref[part, :, first:last].reshape(share * knots, knots)
        right = coupling_ref[part, :, :last].reshape(share * knots, last)
        target_ref[n, :, :last] -= dot_tn(left, right)


def couple(row_ref, inverse_ref, coupling_ref):
    width = coupling_ref.shape[2]
    for n in range(inverse_ref.shape[0]):
        coupling_ref[n] = dot_hi(inverse_ref[n], row_ref[n, :, :width])


def leaf_kernel(basis_ref, turned_ref, prior_ref, *refs, top):
    tier = basis_ref.shape[0] - 1
    leaves = 2 ** (tier - top)
    slot_refs, refs = refs[:leaves], refs[leaves:]
    inverse_ref, coupling_ref, row_ref = refs[:3]
    lower_refs, rest_ref, panel_ref = refs[3:-2], refs[-2], refs[-1]
    knots = basis_ref.shape[2]
    pairs = [ref[...] for ref in slot_refs]
    prior = diagonal(prior_ref[tier:tier + 1, :])
    own = gram_block(basis_ref, turned_ref, pairs, tier, tier)
    for n in range(leaves):
        inverse_ref[n] = own[n * knots:(n + 1) * knots] + prior

    def gram(target_ref, pairs, below, other):
        block = gram_block(basis_ref, turned_ref, pairs, below, other)
        columns = slice(other * knots, (other + 1) * knots)
        for n in range(len(pairs)):
            target_ref[n, :, columns] = block[n * knots:(n + 1) * knots]

    others = [functools.partial(gram, row_ref, pairs, tier, other) for other in range(tier)]
    targets = list(lower_refs) + [rest_ref.at[pl.ds(below, 1)] for below in range(top - 1, -1, -1)]
    for target_ref, below in zip(targets, range(tier - 1, -1, -1)):
        if len(pairs) > 1:
            pairs = [pairs[2 * n] + pairs[2 * n + 1] for n in range(len(pairs) // 2)]
        others += [
            functools.partial(gram, target_ref, pairs, below, other) for other in range(below + 1)
        ]
    for below in range(top - 1):
        rest_ref[below, :, (below + 1) * knots:] = jnp.zeros((knots, (top - 1 - below) * knots), f32)
    invert(
        [inverse_ref.at[n] for n in range(leaves)], [panel_ref.at[n] for n in range(leaves)], others
    )
    couple(row_ref, inverse_ref, coupling_ref)
    update(targets[0], tier - 1, row_ref, coupling_ref)


def forward(source_refs, coupling_ref, target_ref, own_ref, depth):
    nodes, knots, width = coupling_ref.shape
    share = nodes // target_ref.shape[0]
    own_ref[:, depth * knots:(depth + 1) * knots] = source_refs[0][:, width:]
    for n in range(target_ref.shape[0]):
        reduced = [
            source_refs[c][:, :width] - dot_hi(source_refs[c][:, width:], coupling_ref[c])
            for c in range(n * share, (n + 1) * share)
        ]
        target_ref[n] = tree_sum(reduced)


def inner_kernel(*refs, top, count, leaves):
    slot_refs, refs = refs[:leaves], refs[leaves:]
    row_ref, coupling_ref = refs[:2]
    row_refs, (rest_in, prior_ref), refs = refs[2:2 + count], refs[2 + count:4 + count], refs[4 + count:]
    inverse_refs, coupling_refs, refs = refs[:count], refs[count:2 * count], refs[2 * count:]
    (rest_ref, right_ref, own_ref, panel_ref), refs = refs[:4], refs[4:]
    work_refs, reduced_refs = refs[:count], refs[count:]
    knots = prior_ref.shape[1]
    for work_ref, ref in zip(work_refs, row_refs):
        work_ref[...] = ref[...]
    rest_ref[...] = rest_in[...]
    targets = list(work_refs) + [rest_ref.at[pl.ds(below, 1)] for below in range(top - 1, -1, -1)]
    source_refs = slot_refs
    for i in range(count):
        tier = top + count - 1 - i
        nodes = work_refs[i].shape[0]
        prior = diagonal(prior_ref[tier:tier + 1, :])
        for n in range(nodes):
            inverse_refs[i][n] = work_refs[i][n, :, tier * knots:] + prior
        others = [
            functools.partial(update, targets[i + tier - below], below, row_ref, coupling_ref)
            for below in range(tier - 1, -1, -1)
        ]
        others.append(functools.partial(
            forward, source_refs, coupling_ref, reduced_refs[i], own_ref, i
        ))
        invert(
            [inverse_refs[i].at[n] for n in range(nodes)],
            [panel_ref.at[n] for n in range(nodes)],
            others,
        )
        couple(work_refs[i], inverse_refs[i], coupling_refs[i])
        row_ref, coupling_ref = work_refs[i], coupling_refs[i]
        source_refs = [reduced_refs[i].at[n] for n in range(nodes)]
        if i + 1 < count:
            update(targets[i + 1], tier - 1, row_ref, coupling_ref)
    for below in range(top - 1, -1, -1):
        update(targets[count + top - 1 - below], below, row_ref, coupling_ref)
    forward(source_refs, coupling_ref, right_ref, own_ref, count)


def whole_call(kernel, args, shapes, scratch, name, limit=8, flops=10**10):
    return pl.pallas_call(
        kernel,
        in_specs=[vmem] * len(args),
        out_specs=[vmem] * len(shapes),
        out_shape=[jax.ShapeDtypeStruct(shape, f32) for shape in shapes],
        scratch_shapes=[pltpu.VMEM(shape, f32) for shape in scratch],
        compiler_params=pltpu.CompilerParams(vmem_limit_bytes=limit * 2**20),
        cost_estimate=pl.CostEstimate(flops=flops, bytes_accessed=2**20, transcendentals=0),
        name=name,
    )(*args)


def leaf_tier(slots, basis_table, turned, prior_precision, top):
    tier_count, _, knots = basis_table.shape
    tier = tier_count - 1
    leaves = len(slots)
    shapes = [(leaves, knots, knots)] + [(leaves, knots, tier * knots)] * 2
    shapes += [(2 ** (t - top), knots, (t + 1) * knots) for t in range(tier - 1, top - 1, -1)]
    shapes.append((top, knots, top * knots))
    inverse, coupling, row, *lower, rest = whole_call(
        functools.partial(leaf_kernel, top=top),
        (basis_table, turned, prior_precision, *slots),
        shapes, [(leaves, knots, knots)], "leaf_tier", limit=16, flops=2 * 10**10,
    )
    return inverse, coupling, row, lower, rest


def inner_tiers(slots, row, coupling, lower, rest, prior_precision, top):
    knots = prior_precision.shape[1]
    fields = slots[0].shape[0]
    count = len(lower)
    nodes = [value.shape[0] for value in lower]
    shapes = [(n, knots, knots) for n in nodes]
    shapes += [(n, knots, value.shape[2] - knots) for n, value in zip(nodes, lower)]
    shapes += [rest.shape, (1, fields, top * knots), (fields, (count + 1) * knots)]
    scratch = [(max(nodes), knots, knots)] + [value.shape for value in lower]
    scratch += [(n, fields, value.shape[2]) for n, value in zip(nodes, lower)]
    out = whole_call(
        functools.partial(inner_kernel, top=top, count=count, leaves=len(slots)),
        (*slots, row, coupling, *lower, rest, prior_precision),
        shapes, scratch, "inner_tiers", limit=16, flops=2 * 10**10,
    )
    rest = out[-3].reshape(top * knots, top * knots)
    return list(out[:count]), list(out[count:-3]), rest, out[-2][0], out[-1]


def composites(own_ref, refs, local_ref, deep_ref):
    count = len(refs) // 2
    inverse_refs, coupling_refs = refs[:count], refs[count:]
    knots = inverse_refs[0].shape[1]
    wide = deep_ref.shape[1]

    def solve(depth):
        place = slice((count - 1 - depth) * knots, (count - depth) * knots)
        own = own_ref[:, depth * knots:(depth + 1) * knots]
        local_ref[:, place] = dot_hi(own, inverse_refs[depth][0])

    def shorten(depth):
        first = (count - 1 - depth) * knots
        deep = coupling_refs[depth][0, :, :wide]
        if first > 0:
            between = coupling_refs[depth][0, :, wide:]
            deep = deep - dot_hi(between, deep_ref[:first, :])
            local_ref[:, first:first + knots] -= dot_nt(local_ref[:, :first], between, highest)
        deep_ref[first:first + knots, :] = deep

    depths = range(count - 1, -1, -1)
    return [functools.partial(solve, d) for d in depths] + [
        functools.partial(shorten, d) for d in depths
    ]


def top_step(total, prior_row, inverse_ref, panel_ref, others):
    knots = inverse_ref.shape[0]
    row = total[knots:]
    inverse_ref[...] = row[:, knots:] + diagonal(prior_row)
    invert([inverse_ref], [panel_ref], others)
    coupling = dot_hi(inverse_ref[...], row[:, :knots])
    return coupling, total[:knots, :knots] - dot_tn(row[:, :knots], coupling)


def root_step(schur, prior_row, inverse_ref, panel_ref):
    inverse_ref[...] = schur + diagonal(prior_row)
    invert([inverse_ref], [panel_ref])


def top_kernel(rest_ref, other_ref, prior_ref, own_ref, *refs, both):
    refs, outs = refs[:-6], refs[-6:]
    local_ref, deep_ref, top_ref, coupling_ref, last_ref, panel_ref = outs
    coupling_ref[...], schur = top_step(
        rest_ref[...] + other_ref[...], prior_ref[1:2, :], top_ref, panel_ref,
        composites(own_ref, refs, local_ref, deep_ref),
    )
    if both:
        root_step(schur, prior_ref[0:1, :], last_ref, panel_ref)
    else:
        last_ref[...] = schur


def root_kernel(schur_ref, prior_ref, root_ref, panel_ref):
    root_step(schur_ref[...], prior_ref[0:1, :], root_ref, panel_ref)


def right_kernel(right_ref, other_ref, coupling_ref, out_ref):
    knots = coupling_ref.shape[0]
    right = right_ref[...] + other_ref[...]
    out_ref[:, knots:] = right[:, knots:]
    out_ref[:, :knots] = right[:, :knots] - dot_hi(right[:, knots:], coupling_ref[...])


def descend_kernel(right_ref, other_ref, top_ref, coupling_ref, root_ref, local_ref, deep_ref,
                   out_ref, *, reduced):
    knots = top_ref.shape[0]
    right = right_ref[...]
    if reduced:
        root_right = right[:, :knots]
    else:
        right = right + other_ref[...]
        root_right = right[:, :knots] - dot_hi(right[:, knots:], coupling_ref[...])
    first = dot_hi(root_right, root_ref[...])
    second = dot_hi(right[:, knots:], top_ref[...]) - dot_nt(first, coupling_ref[...], highest)
    tops = jnp.concatenate([first, second], axis=1)
    out_ref[:, :2 * knots] = tops
    out_ref[:, 2 * knots:] = local_ref[...] - dot_nt(tops, deep_ref[...], highest)


def path_weights(rest, right, own, prior_precision, inverses, couplings, leaves):
    knots = prior_precision.shape[1]
    fields = right.shape[0]
    square = (knots, knots)
    region_count = lax.axis_size("region")
    other_right = moved(right, leaves, (leaves // 2, 1), (leaves // 2, 1))
    reduced = region_count > leaves
    args = (rest, swapped(rest, "obs", 1), prior_precision, own, *inverses, *couplings)
    shapes = [(fields, own.shape[1]), (own.shape[1], 2 * knots), square, square, square]
    local, deep, top, coupling, root = whole_call(
        functools.partial(top_kernel, both=not reduced), args, shapes, [square], "top"
    )
    if reduced:
        schur = sum_over(root, "region", leaves, region_count)
        root = whole_call(root_kernel, (schur, prior_precision), [square], [square], "root")[0]
        right = whole_call(right_kernel, (right, other_right, coupling), [right.shape], [], "right")[0]
        other_right = sum_over(right[:, :knots], "region", leaves, region_count)
        right = jnp.concatenate([other_right, right[:, knots:]], axis=1)
    args = (right, other_right, top, coupling, root, local, deep)
    shape = (fields, prior_precision.shape[0] * knots)
    kernel = functools.partial(descend_kernel, reduced=reduced)
    return whole_call(kernel, args, [shape], [], "descend", flops=10**9)[0]


def fitted_kernel(pattern_ref, amplitude_ref, weight_ref, turned_ref, out_ref, table):
    tier_count, knots, pattern_count = turned_ref.shape
    field_count = weight_ref.shape[0]

    @pl.when(pl.program_id(0) == 0)
    def _():
        for tier in range(tier_count):
            high, low = split(weight_ref[:, tier * knots:(tier + 1) * knots])
            table[tier * field_count:(tier + 1) * field_count, :] = (
                dot(high, turned_ref[tier]) + dot(low, turned_ref[tier])
            ).astype(bf16)

    picked = dot(table[...], one_hot(pattern_ref[...], pattern_count))
    amp = amplitude_ref[...]
    total = picked[:field_count] * amp[0:1]
    for tier in range(1, tier_count):
        total = total + picked[tier * field_count:(tier + 1) * field_count] * amp[tier:tier + 1]
    out_ref[...] = total


def fitted_fields(pattern, amplitude, weights, turned):
    tier_count, knots, pattern_count = turned.shape
    obs = pattern.shape[0]
    field_count = weights.shape[0]
    block = min(4096, obs)
    return pl.pallas_call(
        fitted_kernel,
        grid=(obs // block,),
        in_specs=[
            pl.BlockSpec((1, block), lambda i: (0, i)),
            pl.BlockSpec((tier_count, block), lambda i: (0, i)),
            pl.BlockSpec(weights.shape, lambda i: (0, 0)),
            pl.BlockSpec(turned.shape, lambda i: (0, 0, 0)),
        ],
        out_specs=pl.BlockSpec((field_count, block), lambda i: (0, i)),
        out_shape=jax.ShapeDtypeStruct((field_count, obs), f32),
        scratch_shapes=[pltpu.VMEM((tier_count * field_count, pattern_count), bf16)],
        compiler_params=pltpu.CompilerParams(vmem_limit_bytes=16 * 2**20),
        name="fitted_fields",
    )(pattern.reshape(1, obs), amplitude, weights, turned)


def swapped(value, axis, mask):
    pairs = [(source, source ^ mask) for source in range(lax.axis_size(axis))]
    return lax.ppermute(value, axis, pairs)


def sum_over(value, axis, first_mask, size):
    mask = first_mask
    while mask < size:
        value = value + swapped(value, axis, mask)
        mask *= 2
    return value


def in_own_half(leaves):
    return (lax.axis_index("region") % leaves) // (leaves // 2) == lax.axis_index("obs") % 2


def moved(value, leaves, own_move, other_move):
    region_count, obs_count = lax.axis_size("region"), lax.axis_size("obs")
    pairs = []
    for region in range(region_count):
        for obs in range(obs_count):
            own = (region % leaves) // (leaves // 2) == obs % 2
            region_mask, obs_mask = own_move if own else other_move
            target = (region ^ region_mask) * obs_count + (obs ^ obs_mask)
            pairs.append((region * obs_count + obs, target))
    return lax.ppermute(value, ("region", "obs"), pairs)


def sum_for_half(value, leaves):
    half = leaves // 2
    parts = lax.axis_size("obs") // 2
    got = [
        moved(value, leaves, (0, 2 * max(offset, 1)), (half, 1 ^ 2 * offset))
        for offset in range(parts)
    ]
    own = value
    for part in got[1:]:
        own = own + part
    other = got[0]
    for part in got[1:]:
        other = other + part
    return jnp.where(in_own_half(leaves), own, other)


def gather_half(value, leaves):
    return [value] + [swapped(value, "region", offset) for offset in range(1, leaves // 2)]


def spread_weights(weights, leaves):
    return jnp.where(in_own_half(leaves), weights, swapped(weights, "obs", 1))


def shards(pattern, amplitude, basis_table, fields, prior_precision):
    tier_count = basis_table.shape[0]
    leaves = 2 ** (tier_count - 2)
    order = tier_count * basis_table.shape[2]
    turned = jnp.swapaxes(basis_table, 1, 2)
    sums = statistics(pattern, amplitude, fields, basis_table)
    pair_rows = sums.shape[0] - fields.shape[0]
    sums = sums + swapped(sums, "obs", 1)
    pairs, project = sums[:pair_rows, :basis_table.shape[1]], sums[pair_rows:, :order]
    pairs = sum_for_half(pairs, leaves)
    project = sum_over(project, "obs", 2, lax.axis_size("obs"))
    pair_slots = gather_half(pairs, leaves)
    project_slots = gather_half(project, leaves)
    inverse, coupling, row, lower, rest = leaf_tier(
        pair_slots, basis_table, turned, prior_precision, 2
    )
    inverses, couplings, rest, right, own = inner_tiers(
        project_slots, row, coupling, lower, rest, prior_precision, 2
    )
    inverses, couplings = [inverse] + inverses, [coupling] + couplings
    weights = path_weights(rest, right, own, prior_precision, inverses, couplings, leaves)
    weights = spread_weights(weights, leaves)
    return fitted_fields(pattern, amplitude, weights, turned)


def solution(mesh):
    return jax.shard_map(
        shards,
        mesh=mesh,
        in_specs=(
            P(("region", "obs")),
            P(None, ("region", "obs")),
            P(),
            P(None, ("region", "obs")),
            P(),
        ),
        out_specs=P(None, ("region", "obs")),
        check_vma=False,
    )
```

```python
import functools

import jax
import jax.numpy as jnp
from jax import lax
from jax.experimental import pallas as pl
from jax.experimental.pallas import tpu as pltpu
from jax.sharding import PartitionSpec as P

highest = lax.Precision.HIGHEST
f32 = jnp.float32
bf16 = jnp.bfloat16
SUB = 8
vmem = pl.BlockSpec(memory_space=pltpu.VMEM)
PANELS = {1: (64, 2), 2: (32, 2)}


def pair_index(tier, other):
    return tier * (tier + 1) // 2 + other


def dot(a, b):
    return jnp.dot(a, b, preferred_element_type=f32)


def dot_nt(a, b, precision=None):
    return lax.dot_general(
        a, b, (((1,), (1,)), ((), ())), precision=precision, preferred_element_type=f32
    )


def dot_tn(a, b):
    return lax.dot_general(
        a, b, (((0,), (0,)), ((), ())), precision=highest, preferred_element_type=f32
    )


def dot_hi(a, b):
    return jnp.dot(a, b, precision=highest, preferred_element_type=f32)


def split(value):
    high = value.astype(bf16)
    return high, (value - high.astype(f32)).astype(bf16)


def split3(value):
    high = value.astype(bf16)
    rest = value - high.astype(f32)
    middle = rest.astype(bf16)
    return high, middle, (rest - middle.astype(f32)).astype(bf16)


def one_hot(pattern_row, pattern_count):
    rows = lax.broadcasted_iota(jnp.int16, (pattern_count, pattern_row.shape[1]), 0)
    return jnp.where(rows == pattern_row.astype(jnp.int16), jnp.asarray(1, bf16), jnp.asarray(0, bf16))


def stats_kernel(pattern_ref, amplitude_ref, fields_ref, basis_ref, out_ref, prods, acc):
    step = pl.program_id(0)
    tier_count, pattern_count, knots = basis_ref.shape
    field_count = fields_ref.shape[0]
    pair_rows = prods.shape[0]
    amp = amplitude_ref[...]
    prods[...] = jnp.zeros_like(prods)
    for tier in range(tier_count):
        first = pair_index(tier, 0)
        prods[first:first + tier + 1, :] = amp[:tier + 1] * amp[tier:tier + 1]
    pair_parts = split3(prods[...])
    plain = fields_ref[...]
    field_rows = plain.astype(f32)
    shifted = amp - 1.0
    values = jnp.concatenate(
        [*pair_parts, plain]
        + [(field_rows * shifted[tier:tier + 1]).astype(bf16) for tier in range(tier_count)],
        axis=0,
    )
    part = dot_nt(values, one_hot(pattern_ref[...], pattern_count))

    @pl.when(step == 0)
    def _():
        acc[...] = part

    @pl.when(step > 0)
    def _():
        acc[...] += part

    @pl.when(step == pl.num_programs(0) - 1)
    def _():
        base = 3 * pair_rows
        out_ref[...] = jnp.zeros_like(out_ref)
        out_ref[:pair_rows, :pattern_count] = acc[:pair_rows] + (
            acc[pair_rows:2 * pair_rows] + acc[2 * pair_rows:base]
        )
        plain_sum = acc[base:base + field_count]
        for tier in range(tier_count):
            first = base + (tier + 1) * field_count
            high, low = split(plain_sum + acc[first:first + field_count])
            out_ref[pair_rows:, tier * knots:(tier + 1) * knots] = (
                dot(high, basis_ref[tier]) + dot(low, basis_ref[tier])
            )


def statistics(pattern, amplitude, fields, basis_table):
    tier_count, pattern_count, knots = basis_table.shape
    field_count, obs = fields.shape
    block = min(8192, obs)
    pair_rows = -(-pair_index(tier_count, 0) // 16) * 16
    rows = 3 * pair_rows + (1 + tier_count) * field_count
    width = max(pattern_count, tier_count * knots)
    return pl.pallas_call(
        stats_kernel,
        grid=(obs // block,),
        in_specs=[
            pl.BlockSpec((1, block), lambda i: (0, i)),
            pl.BlockSpec((tier_count, block), lambda i: (0, i)),
            pl.BlockSpec((field_count, block), lambda i: (0, i)),
            pl.BlockSpec(basis_table.shape, lambda i: (0, 0, 0)),
        ],
        out_specs=pl.BlockSpec((pair_rows + field_count, width), lambda i: (0, 0)),
        out_shape=pltpu.VMEM((pair_rows + field_count, width), f32),
        scratch_shapes=[
            pltpu.VMEM((pair_rows, block), f32),
            pltpu.VMEM((rows, pattern_count), f32),
        ],
        compiler_params=pltpu.CompilerParams(vmem_limit_bytes=58 * 2**20),
        cost_estimate=pl.CostEstimate(
            flops=2 * rows * pattern_count * obs, bytes_accessed=4 * 2**20, transcendentals=0
        ),
        name="statistics",
    )(pattern.reshape(1, obs), amplitude, fields, basis_table)


def along_rows(x, row):
    return jnp.broadcast_to(x[row:row + 1, :], x.shape)


def along_lanes(x, lane):
    return jnp.broadcast_to(x[:, lane:lane + 1], x.shape)


def tree_sum(values):
    while len(values) > 1:
        ends = values[len(values) - len(values) % 2:]
        values = [values[i] + values[i + 1] for i in range(0, len(values) - 1, 2)] + ends
    return values[0]


def sweep(rows, first, group, lane0, sub, lane):
    count, blocks, size = len(rows), len(rows[0]), SUB * group
    here = (lane >= lane0) & (lane < lane0 + size)
    columns, pivot = [], []
    for m in range(count):
        block = rows[m][first:first + group]
        columns.append([[along_lanes(b, lane0 + j) for b in block] for j in range(size)])
        pivot.append([
            jnp.where(here, (lane - lane0 - SUB * a == sub).astype(f32), b)
            for a, b in enumerate(block)
        ])
    for k in range(size):
        at, row = divmod(k, SUB)
        is_row = sub == row
        scale = [
            pltpu.reciprocal(along_rows(columns[m][k][at], row), approx=True) for m in range(count)
        ]

        def eliminated(parts, m):
            scaled = along_rows(parts[at], row) * scale[m]
            out = [part - c * scaled for part, c in zip(parts, columns[m][k])]
            out[at] = jnp.where(is_row, scaled, out[at])
            return out

        for j in range(k + 1, size):
            for m in range(count):
                columns[m][j] = eliminated(columns[m][j], m)
        for m in range(count):
            pivot[m] = eliminated(pivot[m], m)
    solved = [[along_rows(pivot[m][j // SUB], j % SUB) for j in range(size)] for m in range(count)]
    out = [list(r) for r in rows]
    for step in range(blocks - group):
        i = (first + group + step) % blocks
        for m in range(count):
            total = tree_sum([along_lanes(rows[m][i], lane0 + j) * solved[m][j] for j in range(size)])
            out[m][i] = jnp.where(here, 0.0, rows[m][i]) - total
    for m in range(count):
        out[m][first:first + group] = pivot[m]
    return out


def invert(refs, panel_refs, others=()):
    others = list(others)
    size = refs[0].shape[0]
    count = len(refs)
    panel, group = PANELS.get(count, (16, 1))
    panel = min(panel, size)
    blocks = panel // SUB
    steps = size // (SUB * group)
    each = -(-len(others) // steps)
    sub = lax.broadcasted_iota(jnp.int32, (SUB, size), 0)
    lane = lax.broadcasted_iota(jnp.int32, (SUB, size), 1)
    wide = lax.broadcasted_iota(jnp.int32, (size, size), 1)
    for m in range(count):
        panel_refs[m][...] = jnp.zeros((size, size), f32)
    for p in range(size // panel):
        first = p * panel
        rows = [
            [refs[m][first + SUB * i:first + SUB * (i + 1), :] for i in range(blocks)]
            for m in range(count)
        ]
        for q in range(0, blocks, group):
            for work in others[:each]:
                work()
            others = others[each:]
            rows = sweep(rows, q, group, first + SUB * q, sub, lane)
        for m in range(count):
            if p > 0:
                panel_refs[m][first - panel:first, :] = jnp.zeros((panel, size), f32)
            for i in range(blocks):
                panel_refs[m][first + SUB * i:first + SUB * (i + 1), :] = rows[m][i]
        old = [refs[m][...] for m in range(count)]
        change = [dot_hi(old[m], panel_refs[m][...]) for m in range(count)]
        here = (wide >= first) & (wide < first + panel)
        for m in range(count):
            refs[m][...] = jnp.where(here, 0.0, old[m]) - change[m]
            for i in range(blocks):
                refs[m][first + SUB * i:first + SUB * (i + 1), :] = rows[m][i]


def diagonal(row):
    size = row.shape[1]
    rows = lax.broadcasted_iota(jnp.int32, (size, size), 0)
    columns = lax.broadcasted_iota(jnp.int32, (size, size), 1)
    return jnp.where(rows == columns, row, 0.0)


def gram_block(basis_ref, turned_ref, pairs, tier, other):
    turned = turned_ref[tier].astype(f32)
    index = pair_index(tier, other)
    parts = zip(*[split3(turned * pair[index:index + 1, :]) for pair in pairs])
    product = dot(jnp.concatenate(sum(parts, ()), axis=0), basis_ref[other])
    size = len(pairs) * turned.shape[0]
    return product[:size] + (product[size:2 * size] + product[2 * size:])


def update(target_ref, below, row_ref, coupling_ref, begin=0, end=None):
    nodes, knots = row_ref.shape[:2]
    share = nodes // target_ref.shape[0]
    first, last = below * knots, (below + 1) * knots
    end = last if end is None else end
    for n in range(target_ref.shape[0]):
        part = slice(n * share, (n + 1) * share)
        left = row_ref[part, :, first:last].reshape(share * knots, knots)
        right = coupling_ref[part, :, begin:end].reshape(share * knots, end - begin)
        target_ref[n, :, begin:end] -= dot_tn(left, right)


def couple(row_ref, inverse_ref, coupling_ref, begin, end):
    for n in range(inverse_ref.shape[0]):
        coupling_ref[n, :, begin:end] = dot_hi(inverse_ref[n], row_ref[n, :, begin:end])


def leaf_kernel(basis_ref, turned_ref, prior_ref, *refs, top):
    tier = basis_ref.shape[0] - 1
    leaves = 2 ** (tier - top)
    slot_refs, refs = refs[:leaves], refs[leaves:]
    inverse_ref, coupling_ref, row_ref = refs[:3]
    lower_refs, rest_ref, panel_ref = refs[3:-2], refs[-2], refs[-1]
    knots = basis_ref.shape[2]
    pairs = [ref[...] for ref in slot_refs]
    prior = diagonal(prior_ref[tier:tier + 1, :])
    own = gram_block(basis_ref, turned_ref, pairs, tier, tier)
    for n in range(leaves):
        inverse_ref[n] = own[n * knots:(n + 1) * knots] + prior

    def gram(target_ref, pairs, below, other):
        block = gram_block(basis_ref, turned_ref, pairs, below, other)
        columns = slice(other * knots, (other + 1) * knots)
        for n in range(len(pairs)):
            target_ref[n, :, columns] = block[n * knots:(n + 1) * knots]

    others = [functools.partial(gram, row_ref, pairs, tier, other) for other in range(tier)]
    targets = list(lower_refs) + [rest_ref.at[pl.ds(below, 1)] for below in range(top - 1, -1, -1)]
    for target_ref, below in zip(targets, range(tier - 1, -1, -1)):
        if len(pairs) > 1:
            pairs = [pairs[2 * n] + pairs[2 * n + 1] for n in range(len(pairs) // 2)]
        others += [
            functools.partial(gram, target_ref, pairs, below, other) for other in range(below + 1)
        ]
    for below in range(top - 1):
        rest_ref[below, :, (below + 1) * knots:] = jnp.zeros((knots, (top - 1 - below) * knots), f32)
    invert(
        [inverse_ref.at[n] for n in range(leaves)], [panel_ref.at[n] for n in range(leaves)], others
    )
    first, last = (tier - 1) * knots, tier * knots
    couple(row_ref, inverse_ref, coupling_ref, first, last)
    update(targets[0], tier - 1, row_ref, coupling_ref, first, last)


def forward(source_refs, coupling_ref, target_ref, own_ref, depth):
    nodes, knots, width = coupling_ref.shape
    share = nodes // target_ref.shape[0]
    own_ref[:, depth * knots:(depth + 1) * knots] = source_refs[0][:, width:]
    for n in range(target_ref.shape[0]):
        reduced = [
            source_refs[c][:, :width] - dot_hi(source_refs[c][:, width:], coupling_ref[c])
            for c in range(n * share, (n + 1) * share)
        ]
        target_ref[n] = tree_sum(reduced)


def inner_kernel(*refs, top, count, leaves):
    slot_refs, refs = refs[:leaves], refs[leaves:]
    row_ref, inverse_ref, coupling_in = refs[:3]
    row_refs, (rest_in, prior_ref), refs = refs[3:3 + count], refs[3 + count:5 + count], refs[5 + count:]
    coupling_ref, refs = refs[0], refs[1:]
    inverse_refs, coupling_refs, refs = refs[:count], refs[count:2 * count], refs[2 * count:]
    (rest_ref, right_ref, own_ref, panel_ref), refs = refs[:4], refs[4:]
    work_refs, reduced_refs = refs[:count], refs[count:]
    knots = prior_ref.shape[1]
    for work_ref, ref in zip(work_refs, row_refs):
        work_ref[...] = ref[...]
    rest_ref[...] = rest_in[...]
    targets = list(work_refs) + [rest_ref.at[pl.ds(below, 1)] for below in range(top - 1, -1, -1)]
    source_refs = slot_refs
    last = coupling_in.shape[2]
    coupling_ref[:, :, last - knots:] = coupling_in[:, :, last - knots:]
    for i in range(count):
        tier = top + count - 1 - i
        nodes = work_refs[i].shape[0]
        prior = diagonal(prior_ref[tier:tier + 1, :])
        for n in range(nodes):
            inverse_refs[i][n] = work_refs[i][n, :, tier * knots:] + prior
        others = [
            functools.partial(couple, row_ref, inverse_ref, coupling_ref, 0, tier * knots),
            functools.partial(
                update, targets[i], tier, row_ref, coupling_ref, 0, tier * knots
            ),
        ]
        others += [
            functools.partial(update, targets[i + tier - below], below, row_ref, coupling_ref)
            for below in range(tier - 1, -1, -1)
        ]
        others.append(functools.partial(
            forward, source_refs, coupling_ref, reduced_refs[i], own_ref, i
        ))
        invert(
            [inverse_refs[i].at[n] for n in range(nodes)],
            [panel_ref.at[n] for n in range(nodes)],
            others,
        )
        row_ref, inverse_ref, coupling_ref = work_refs[i], inverse_refs[i], coupling_refs[i]
        first = (tier - 1) * knots if i + 1 < count else 0
        couple(row_ref, inverse_ref, coupling_ref, first, tier * knots)
        source_refs = [reduced_refs[i].at[n] for n in range(nodes)]
        if i + 1 < count:
            update(targets[i + 1], tier - 1, row_ref, coupling_ref, first, tier * knots)
    for below in range(top - 1, -1, -1):
        update(targets[count + top - 1 - below], below, row_ref, coupling_ref)
    forward(source_refs, coupling_ref, right_ref, own_ref, count)


def whole_call(kernel, args, shapes, scratch, name, limit=8, flops=10**10):
    return pl.pallas_call(
        kernel,
        in_specs=[vmem] * len(args),
        out_specs=[vmem] * len(shapes),
        out_shape=[jax.ShapeDtypeStruct(shape, f32) for shape in shapes],
        scratch_shapes=[pltpu.VMEM(shape, f32) for shape in scratch],
        compiler_params=pltpu.CompilerParams(vmem_limit_bytes=limit * 2**20),
        cost_estimate=pl.CostEstimate(flops=flops, bytes_accessed=2**20, transcendentals=0),
        name=name,
    )(*args)


def leaf_tier(slots, basis_table, turned, prior_precision, top):
    tier_count, _, knots = basis_table.shape
    tier = tier_count - 1
    leaves = len(slots)
    shapes = [(leaves, knots, knots)] + [(leaves, knots, tier * knots)] * 2
    shapes += [(2 ** (t - top), knots, (t + 1) * knots) for t in range(tier - 1, top - 1, -1)]
    shapes.append((top, knots, top * knots))
    inverse, coupling, row, *lower, rest = whole_call(
        functools.partial(leaf_kernel, top=top),
        (basis_table, turned, prior_precision, *slots),
        shapes, [(leaves, knots, knots)], "leaf_tier", limit=16, flops=2 * 10**10,
    )
    return inverse, coupling, row, lower, rest


def inner_tiers(slots, row, inverse, coupling, lower, rest, prior_precision, top):
    knots = prior_precision.shape[1]
    fields = slots[0].shape[0]
    count = len(lower)
    nodes = [value.shape[0] for value in lower]
    shapes = [coupling.shape] + [(n, knots, knots) for n in nodes]
    shapes += [(n, knots, value.shape[2] - knots) for n, value in zip(nodes, lower)]
    shapes += [rest.shape, (1, fields, top * knots), (fields, (count + 1) * knots)]
    scratch = [(max(nodes), knots, knots)] + [value.shape for value in lower]
    scratch += [(n, fields, value.shape[2]) for n, value in zip(nodes, lower)]
    out = whole_call(
        functools.partial(inner_kernel, top=top, count=count, leaves=len(slots)),
        (*slots, row, inverse, coupling, *lower, rest, prior_precision),
        shapes, scratch, "inner_tiers", limit=16, flops=2 * 10**10,
    )
    rest = out[-3].reshape(top * knots, top * knots)
    inverses, couplings = [inverse, *out[1:count + 1]], [out[0], *out[count + 1:-3]]
    return inverses, couplings, rest, out[-2][0], out[-1]


def composites(own_ref, refs, local_ref, deep_ref):
    count = len(refs) // 2
    inverse_refs, coupling_refs = refs[:count], refs[count:]
    knots = inverse_refs[0].shape[1]
    wide = deep_ref.shape[1]

    def solve(depth):
        place = slice((count - 1 - depth) * knots, (count - depth) * knots)
        own = own_ref[:, depth * knots:(depth + 1) * knots]
        local_ref[:, place] = dot_hi(own, inverse_refs[depth][0])

    def shorten(depth):
        first = (count - 1 - depth) * knots
        deep = coupling_refs[depth][0, :, :wide]
        if first > 0:
            between = coupling_refs[depth][0, :, wide:]
            deep = deep - dot_hi(between, deep_ref[:first, :])
            local_ref[:, first:first + knots] -= dot_nt(local_ref[:, :first], between, highest)
        deep_ref[first:first + knots, :] = deep

    depths = range(count - 1, -1, -1)
    return [functools.partial(solve, d) for d in depths] + [
        functools.partial(shorten, d) for d in depths
    ]


def top_step(total, prior_row, inverse_ref, panel_ref, others):
    knots = inverse_ref.shape[0]
    row = total[knots:]
    inverse_ref[...] = row[:, knots:] + diagonal(prior_row)
    invert([inverse_ref], [panel_ref], others)
    coupling = dot_hi(inverse_ref[...], row[:, :knots])
    return coupling, total[:knots, :knots] - dot_tn(row[:, :knots], coupling)


def root_step(schur, prior_row, inverse_ref, panel_ref):
    inverse_ref[...] = schur + diagonal(prior_row)
    invert([inverse_ref], [panel_ref])


def top_kernel(rest_ref, other_ref, prior_ref, own_ref, *refs, both):
    refs, outs = refs[:-6], refs[-6:]
    local_ref, deep_ref, top_ref, coupling_ref, last_ref, panel_ref = outs
    coupling_ref[...], schur = top_step(
        rest_ref[...] + other_ref[...], prior_ref[1:2, :], top_ref, panel_ref,
        composites(own_ref, refs, local_ref, deep_ref),
    )
    if both:
        root_step(schur, prior_ref[0:1, :], last_ref, panel_ref)
    else:
        last_ref[...] = schur


def root_kernel(schur_ref, prior_ref, root_ref, panel_ref):
    root_step(schur_ref[...], prior_ref[0:1, :], root_ref, panel_ref)


def right_kernel(right_ref, other_ref, coupling_ref, out_ref):
    knots = coupling_ref.shape[0]
    right = right_ref[...] + other_ref[...]
    out_ref[:, knots:] = right[:, knots:]
    out_ref[:, :knots] = right[:, :knots] - dot_hi(right[:, knots:], coupling_ref[...])


def descend_kernel(right_ref, other_ref, top_ref, coupling_ref, root_ref, local_ref, deep_ref,
                   out_ref, *, reduced):
    knots = top_ref.shape[0]
    right = right_ref[...]
    if reduced:
        root_right = right[:, :knots]
    else:
        right = right + other_ref[...]
        root_right = right[:, :knots] - dot_hi(right[:, knots:], coupling_ref[...])
    first = dot_hi(root_right, root_ref[...])
    second = dot_hi(right[:, knots:], top_ref[...]) - dot_nt(first, coupling_ref[...], highest)
    tops = jnp.concatenate([first, second], axis=1)
    out_ref[:, :2 * knots] = tops
    out_ref[:, 2 * knots:] = local_ref[...] - dot_nt(tops, deep_ref[...], highest)


def path_weights(rest, right, own, prior_precision, inverses, couplings, leaves):
    knots = prior_precision.shape[1]
    fields = right.shape[0]
    square = (knots, knots)
    region_count = lax.axis_size("region")
    other_right = moved(right, leaves, (leaves // 2, 1), (leaves // 2, 1))
    reduced = region_count > leaves
    args = (rest, swapped(rest, "obs", 1), prior_precision, own, *inverses, *couplings)
    shapes = [(fields, own.shape[1]), (own.shape[1], 2 * knots), square, square, square]
    local, deep, top, coupling, root = whole_call(
        functools.partial(top_kernel, both=not reduced), args, shapes, [square], "top"
    )
    if reduced:
        schur = sum_over(root, "region", leaves, region_count)
        root = whole_call(root_kernel, (schur, prior_precision), [square], [square], "root")[0]
        right = whole_call(right_kernel, (right, other_right, coupling), [right.shape], [], "right")[0]
        other_right = sum_over(right[:, :knots], "region", leaves, region_count)
        right = jnp.concatenate([other_right, right[:, knots:]], axis=1)
    args = (right, other_right, top, coupling, root, local, deep)
    shape = (fields, prior_precision.shape[0] * knots)
    kernel = functools.partial(descend_kernel, reduced=reduced)
    return whole_call(kernel, args, [shape], [], "descend", flops=10**9)[0]


def fitted_kernel(pattern_ref, amplitude_ref, weight_ref, turned_ref, out_ref, table):
    tier_count, knots, pattern_count = turned_ref.shape
    field_count = weight_ref.shape[0]

    @pl.when(pl.program_id(0) == 0)
    def _():
        for tier in range(tier_count):
            high, low = split(weight_ref[:, tier * knots:(tier + 1) * knots])
            table[tier * field_count:(tier + 1) * field_count, :] = (
                dot(high, turned_ref[tier]) + dot(low, turned_ref[tier])
            ).astype(bf16)

    picked = dot(table[...], one_hot(pattern_ref[...], pattern_count))
    amp = amplitude_ref[...]
    total = picked[:field_count] * amp[0:1]
    for tier in range(1, tier_count):
        total = total + picked[tier * field_count:(tier + 1) * field_count] * amp[tier:tier + 1]
    out_ref[...] = total


def fitted_fields(pattern, amplitude, weights, turned):
    tier_count, knots, pattern_count = turned.shape
    obs = pattern.shape[0]
    field_count = weights.shape[0]
    block = min(4096, obs)
    return pl.pallas_call(
        fitted_kernel,
        grid=(obs // block,),
        in_specs=[
            pl.BlockSpec((1, block), lambda i: (0, i)),
            pl.BlockSpec((tier_count, block), lambda i: (0, i)),
            pl.BlockSpec(weights.shape, lambda i: (0, 0)),
            pl.BlockSpec(turned.shape, lambda i: (0, 0, 0)),
        ],
        out_specs=pl.BlockSpec((field_count, block), lambda i: (0, i)),
        out_shape=jax.ShapeDtypeStruct((field_count, obs), f32),
        scratch_shapes=[pltpu.VMEM((tier_count * field_count, pattern_count), bf16)],
        compiler_params=pltpu.CompilerParams(vmem_limit_bytes=16 * 2**20),
        name="fitted_fields",
    )(pattern.reshape(1, obs), amplitude, weights, turned)


def swapped(value, axis, mask):
    pairs = [(source, source ^ mask) for source in range(lax.axis_size(axis))]
    return lax.ppermute(value, axis, pairs)


def sum_over(value, axis, first_mask, size):
    mask = first_mask
    while mask < size:
        value = value + swapped(value, axis, mask)
        mask *= 2
    return value


def in_own_half(leaves):
    return (lax.axis_index("region") % leaves) // (leaves // 2) == lax.axis_index("obs") % 2


def moved(value, leaves, own_move, other_move):
    region_count, obs_count = lax.axis_size("region"), lax.axis_size("obs")
    pairs = []
    for region in range(region_count):
        for obs in range(obs_count):
            own = (region % leaves) // (leaves // 2) == obs % 2
            region_mask, obs_mask = own_move if own else other_move
            target = (region ^ region_mask) * obs_count + (obs ^ obs_mask)
            pairs.append((region * obs_count + obs, target))
    return lax.ppermute(value, ("region", "obs"), pairs)


def sum_for_half(value, leaves):
    half = leaves // 2
    parts = lax.axis_size("obs") // 2
    got = [
        moved(value, leaves, (0, 2 * max(offset, 1)), (half, 1 ^ 2 * offset))
        for offset in range(parts)
    ]
    own = value
    for part in got[1:]:
        own = own + part
    other = got[0]
    for part in got[1:]:
        other = other + part
    return jnp.where(in_own_half(leaves), own, other)


def gather_half(value, leaves):
    return [value] + [swapped(value, "region", offset) for offset in range(1, leaves // 2)]


def spread_weights(weights, leaves):
    return jnp.where(in_own_half(leaves), weights, swapped(weights, "obs", 1))


def shards(pattern, amplitude, basis_table, fields, prior_precision):
    tier_count = basis_table.shape[0]
    leaves = 2 ** (tier_count - 2)
    order = tier_count * basis_table.shape[2]
    turned = jnp.swapaxes(basis_table, 1, 2)
    sums = statistics(pattern, amplitude, fields, basis_table)
    pair_rows = sums.shape[0] - fields.shape[0]
    sums = sums + swapped(sums, "obs", 1)
    pairs, project = sums[:pair_rows, :basis_table.shape[1]], sums[pair_rows:, :order]
    pairs = sum_for_half(pairs, leaves)
    project = sum_over(project, "obs", 2, lax.axis_size("obs"))
    pair_slots = gather_half(pairs, leaves)
    project_slots = gather_half(project, leaves)
    inverse, coupling, row, lower, rest = leaf_tier(
        pair_slots, basis_table, turned, prior_precision, 2
    )
    inverses, couplings, rest, right, own = inner_tiers(
        project_slots, row, inverse, coupling, lower, rest, prior_precision, 2
    )
    weights = path_weights(rest, right, own, prior_precision, inverses, couplings, leaves)
    weights = spread_weights(weights, leaves)
    return fitted_fields(pattern, amplitude, weights, turned)


def solution(mesh):
    return jax.shard_map(
        shards,
        mesh=mesh,
        in_specs=(
            P(("region", "obs")),
            P(None, ("region", "obs")),
            P(),
            P(None, ("region", "obs")),
            P(),
        ),
        out_specs=P(None, ("region", "obs")),
        check_vma=False,
    )
```

```python
import functools

import jax
import jax.numpy as jnp
from jax import lax
from jax.experimental import pallas as pl
from jax.experimental.pallas import tpu as pltpu
from jax.sharding import PartitionSpec as P

highest = lax.Precision.HIGHEST
f32 = jnp.float32
bf16 = jnp.bfloat16
SUB = 8
vmem = pl.BlockSpec(memory_space=pltpu.VMEM)
PANELS = {1: (64, 2), 2: (32, 2)}


def pair_index(tier, other):
    return tier * (tier + 1) // 2 + other


def dot(a, b):
    return jnp.dot(a, b, preferred_element_type=f32)


def dot_nt(a, b, precision=None):
    return lax.dot_general(
        a, b, (((1,), (1,)), ((), ())), precision=precision, preferred_element_type=f32
    )


def dot_tn(a, b):
    return lax.dot_general(
        a, b, (((0,), (0,)), ((), ())), precision=highest, preferred_element_type=f32
    )


def dot_hi(a, b):
    return jnp.dot(a, b, precision=highest, preferred_element_type=f32)


def split(value):
    high = value.astype(bf16)
    return high, (value - high.astype(f32)).astype(bf16)


def split3(value):
    high = value.astype(bf16)
    rest = value - high.astype(f32)
    middle = rest.astype(bf16)
    return high, middle, (rest - middle.astype(f32)).astype(bf16)


def one_hot(pattern_row, pattern_count):
    rows = lax.broadcasted_iota(jnp.int16, (pattern_count, pattern_row.shape[1]), 0)
    return jnp.where(rows == pattern_row.astype(jnp.int16), jnp.asarray(1, bf16), jnp.asarray(0, bf16))


def stats_kernel(pattern_ref, amplitude_ref, fields_ref, basis_ref, out_ref, prods, acc):
    step = pl.program_id(0)
    tier_count, pattern_count, knots = basis_ref.shape
    field_count = fields_ref.shape[0]
    pair_rows = prods.shape[0]
    amp = amplitude_ref[...]
    prods[...] = jnp.zeros_like(prods)
    for tier in range(tier_count):
        first = pair_index(tier, 0)
        prods[first:first + tier + 1, :] = amp[:tier + 1] * amp[tier:tier + 1]
    pair_parts = split3(prods[...])
    plain = fields_ref[...]
    field_rows = plain.astype(f32)
    shifted = amp - 1.0
    values = jnp.concatenate(
        [*pair_parts, plain]
        + [(field_rows * shifted[tier:tier + 1]).astype(bf16) for tier in range(tier_count)],
        axis=0,
    )
    part = dot_nt(values, one_hot(pattern_ref[...], pattern_count))

    @pl.when(step == 0)
    def _():
        acc[...] = part

    @pl.when(step > 0)
    def _():
        acc[...] += part

    @pl.when(step == pl.num_programs(0) - 1)
    def _():
        base = 3 * pair_rows
        out_ref[...] = jnp.zeros_like(out_ref)
        out_ref[:pair_rows, :pattern_count] = acc[:pair_rows] + (
            acc[pair_rows:2 * pair_rows] + acc[2 * pair_rows:base]
        )
        plain_sum = acc[base:base + field_count]
        for tier in range(tier_count):
            first = base + (tier + 1) * field_count
            high, low = split(plain_sum + acc[first:first + field_count])
            out_ref[pair_rows:, tier * knots:(tier + 1) * knots] = (
                dot(high, basis_ref[tier]) + dot(low, basis_ref[tier])
            )


def statistics(pattern, amplitude, fields, basis_table):
    tier_count, pattern_count, knots = basis_table.shape
    field_count, obs = fields.shape
    block = min(8192, obs)
    pair_rows = -(-pair_index(tier_count, 0) // 16) * 16
    rows = 3 * pair_rows + (1 + tier_count) * field_count
    width = max(pattern_count, tier_count * knots)
    return pl.pallas_call(
        stats_kernel,
        grid=(obs // block,),
        in_specs=[
            pl.BlockSpec((1, block), lambda i: (0, i)),
            pl.BlockSpec((tier_count, block), lambda i: (0, i)),
            pl.BlockSpec((field_count, block), lambda i: (0, i)),
            pl.BlockSpec(basis_table.shape, lambda i: (0, 0, 0)),
        ],
        out_specs=pl.BlockSpec((pair_rows + field_count, width), lambda i: (0, 0)),
        out_shape=pltpu.VMEM((pair_rows + field_count, width), f32),
        scratch_shapes=[
            pltpu.VMEM((pair_rows, block), f32),
            pltpu.VMEM((rows, pattern_count), f32),
        ],
        compiler_params=pltpu.CompilerParams(vmem_limit_bytes=58 * 2**20),
        cost_estimate=pl.CostEstimate(
            flops=2 * rows * pattern_count * obs, bytes_accessed=4 * 2**20, transcendentals=0
        ),
        name="statistics",
    )(pattern.reshape(1, obs), amplitude, fields, basis_table)


def along_rows(x, row):
    return jnp.broadcast_to(x[row:row + 1, :], x.shape)


def along_lanes(x, lane):
    return jnp.broadcast_to(x[:, lane:lane + 1], x.shape)


def tree_sum(values):
    while len(values) > 1:
        ends = values[len(values) - len(values) % 2:]
        values = [values[i] + values[i + 1] for i in range(0, len(values) - 1, 2)] + ends
    return values[0]


def sweep(rows, first, group, lane0, sub, lane):
    count, blocks, size = len(rows), len(rows[0]), SUB * group
    here = (lane >= lane0) & (lane < lane0 + size)
    columns, pivot = [], []
    for m in range(count):
        block = rows[m][first:first + group]
        columns.append([[along_lanes(b, lane0 + j) for b in block] for j in range(size)])
        pivot.append([
            jnp.where(here, (lane - lane0 - SUB * a == sub).astype(f32), b)
            for a, b in enumerate(block)
        ])
    for k in range(size):
        at, row = divmod(k, SUB)
        is_row = sub == row
        scale = [
            pltpu.reciprocal(along_rows(columns[m][k][at], row), approx=True) for m in range(count)
        ]

        def eliminated(parts, m):
            scaled = along_rows(parts[at], row) * scale[m]
            out = [part - c * scaled for part, c in zip(parts, columns[m][k])]
            out[at] = jnp.where(is_row, scaled, out[at])
            return out

        for j in range(k + 1, size):
            for m in range(count):
                columns[m][j] = eliminated(columns[m][j], m)
        for m in range(count):
            pivot[m] = eliminated(pivot[m], m)
    solved = [[along_rows(pivot[m][j // SUB], j % SUB) for j in range(size)] for m in range(count)]
    out = [list(r) for r in rows]
    for step in range(blocks - group):
        i = (first + group + step) % blocks
        for m in range(count):
            total = tree_sum([along_lanes(rows[m][i], lane0 + j) * solved[m][j] for j in range(size)])
            out[m][i] = jnp.where(here, 0.0, rows[m][i]) - total
    for m in range(count):
        out[m][first:first + group] = pivot[m]
    return out


def invert(refs, panel_refs, others=()):
    others = list(others)
    size = refs[0].shape[0]
    count = len(refs)
    panel, group = PANELS.get(count, (16, 1))
    panel = min(panel, size)
    blocks = panel // SUB
    steps = size // (SUB * group)
    each = -(-len(others) // steps)
    sub = lax.broadcasted_iota(jnp.int32, (SUB, size), 0)
    lane = lax.broadcasted_iota(jnp.int32, (SUB, size), 1)
    wide = lax.broadcasted_iota(jnp.int32, (size, size), 1)
    for m in range(count):
        panel_refs[m][...] = jnp.zeros((size, size), f32)
    for p in range(size // panel):
        first = p * panel
        rows = [
            [refs[m][first + SUB * i:first + SUB * (i + 1), :] for i in range(blocks)]
            for m in range(count)
        ]
        for q in range(0, blocks, group):
            for work in others[:each]:
                work()
            others = others[each:]
            rows = sweep(rows, q, group, first + SUB * q, sub, lane)
        for m in range(count):
            if p > 0:
                panel_refs[m][first - panel:first, :] = jnp.zeros((panel, size), f32)
            for i in range(blocks):
                panel_refs[m][first + SUB * i:first + SUB * (i + 1), :] = rows[m][i]
        old = [refs[m][...] for m in range(count)]
        change = [dot_hi(old[m], panel_refs[m][...]) for m in range(count)]
        here = (wide >= first) & (wide < first + panel)
        for m in range(count):
            refs[m][...] = jnp.where(here, 0.0, old[m]) - change[m]
            for i in range(blocks):
                refs[m][first + SUB * i:first + SUB * (i + 1), :] = rows[m][i]


def diagonal(row):
    size = row.shape[1]
    rows = lax.broadcasted_iota(jnp.int32, (size, size), 0)
    columns = lax.broadcasted_iota(jnp.int32, (size, size), 1)
    return jnp.where(rows == columns, row, 0.0)


def gram_block(basis_ref, turned_ref, pairs, tier, other):
    turned = turned_ref[tier].astype(f32)
    index = pair_index(tier, other)
    parts = zip(*[split3(turned * pair[index:index + 1, :]) for pair in pairs])
    product = dot(jnp.concatenate(sum(parts, ()), axis=0), basis_ref[other])
    size = len(pairs) * turned.shape[0]
    return product[:size] + (product[size:2 * size] + product[2 * size:])


def update(target_ref, below, row_ref, coupling_ref, begin=0, end=None):
    nodes, knots = row_ref.shape[:2]
    share = nodes // target_ref.shape[0]
    first, last = below * knots, (below + 1) * knots
    end = last if end is None else end
    for n in range(target_ref.shape[0]):
        part = slice(n * share, (n + 1) * share)
        left = row_ref[part, :, first:last].reshape(share * knots, knots)
        right = coupling_ref[part, :, begin:end].reshape(share * knots, end - begin)
        target_ref[n, :, begin:end] -= dot_tn(left, right)


def couple(row_ref, inverse_ref, coupling_ref, begin, end, nodes=None):
    for n in nodes or range(inverse_ref.shape[0]):
        coupling_ref[n, :, begin:end] = dot_hi(inverse_ref[n], row_ref[n, :, begin:end])


def leaf_kernel(basis_ref, turned_ref, prior_ref, *refs, top):
    tier = basis_ref.shape[0] - 1
    leaves = 2 ** (tier - top)
    slot_refs, refs = refs[:leaves], refs[leaves:]
    inverse_ref, coupling_ref, row_ref = refs[:3]
    lower_refs, rest_ref, panel_ref = refs[3:-2], refs[-2], refs[-1]
    knots = basis_ref.shape[2]
    pairs = [ref[...] for ref in slot_refs]
    prior = diagonal(prior_ref[tier:tier + 1, :])
    own = gram_block(basis_ref, turned_ref, pairs, tier, tier)
    for n in range(leaves):
        inverse_ref[n] = own[n * knots:(n + 1) * knots] + prior

    def gram(target_ref, pairs, below, other):
        block = gram_block(basis_ref, turned_ref, pairs, below, other)
        columns = slice(other * knots, (other + 1) * knots)
        for n in range(len(pairs)):
            target_ref[n, :, columns] = block[n * knots:(n + 1) * knots]

    others = [functools.partial(gram, row_ref, pairs, tier, other) for other in range(tier)]
    targets = list(lower_refs) + [rest_ref.at[pl.ds(below, 1)] for below in range(top - 1, -1, -1)]
    for target_ref, below in zip(targets, range(tier - 1, -1, -1)):
        if len(pairs) > 1:
            pairs = [pairs[2 * n] + pairs[2 * n + 1] for n in range(len(pairs) // 2)]
        others += [
            functools.partial(gram, target_ref, pairs, below, other) for other in range(below + 1)
        ]
    for below in range(top - 1):
        rest_ref[below, :, (below + 1) * knots:] = jnp.zeros((knots, (top - 1 - below) * knots), f32)
    invert(
        [inverse_ref.at[n] for n in range(leaves)], [panel_ref.at[n] for n in range(leaves)], others
    )
    first, last = (tier - 1) * knots, tier * knots
    couple(row_ref, inverse_ref, coupling_ref, first, last)
    update(targets[0], tier - 1, row_ref, coupling_ref, first, last)


def forward(source_refs, coupling_ref, target_ref, own_ref, depth, targets):
    nodes, knots, width = coupling_ref.shape
    share = nodes // target_ref.shape[0]
    if 0 in targets:
        own_ref[:, depth * knots:(depth + 1) * knots] = source_refs[0][:, width:]
    for n in targets:
        reduced = [
            source_refs[c][:, :width] - dot_hi(source_refs[c][:, width:], coupling_ref[c])
            for c in range(n * share, (n + 1) * share)
        ]
        target_ref[n] = tree_sum(reduced)


def inner_kernel(*refs, top, count, leaves):
    slot_refs, refs = refs[:leaves], refs[leaves:]
    row_ref, inverse_ref, coupling_in = refs[:3]
    row_refs, (rest_in, prior_ref), refs = refs[3:3 + count], refs[3 + count:5 + count], refs[5 + count:]
    coupling_ref, refs = refs[0], refs[1:]
    inverse_refs, coupling_refs, refs = refs[:count], refs[count:2 * count], refs[2 * count:]
    (rest_ref, right_ref, own_ref, panel_ref), refs = refs[:4], refs[4:]
    work_refs, reduced_refs = refs[:count], refs[count:]
    knots = prior_ref.shape[1]
    for work_ref, ref in zip(work_refs, row_refs):
        work_ref[...] = ref[...]
    rest_ref[...] = rest_in[...]
    targets = list(work_refs) + [rest_ref.at[pl.ds(below, 1)] for below in range(top - 1, -1, -1)]
    source_refs = slot_refs
    last = coupling_in.shape[2]
    coupling_ref[:, :, last - knots:] = coupling_in[:, :, last - knots:]
    for i in range(count):
        tier = top + count - 1 - i
        nodes = work_refs[i].shape[0]
        prior = diagonal(prior_ref[tier:tier + 1, :])
        for n in range(nodes):
            inverse_refs[i][n] = work_refs[i][n, :, tier * knots:] + prior
        above = inverse_ref.shape[0]
        others = [
            functools.partial(
                couple, row_ref, inverse_ref, coupling_ref, 0, tier * knots, part
            )
            for part in (range(above // 2), range(above // 2, above))
        ]
        others += [
            functools.partial(
                update, targets[i], tier, row_ref, coupling_ref, 0, tier * knots
            ),
        ]
        others += [
            functools.partial(update, targets[i + tier - below], below, row_ref, coupling_ref)
            for below in range(tier - 1, -1, -1)
        ]
        others += [
            functools.partial(
                forward, source_refs, coupling_ref, reduced_refs[i], own_ref, i, [n]
            )
            for n in range(nodes)
        ]
        invert(
            [inverse_refs[i].at[n] for n in range(nodes)],
            [panel_ref.at[n] for n in range(nodes)],
            others,
        )
        row_ref, inverse_ref, coupling_ref = work_refs[i], inverse_refs[i], coupling_refs[i]
        first = (tier - 1) * knots if i + 1 < count else 0
        couple(row_ref, inverse_ref, coupling_ref, first, tier * knots)
        source_refs = [reduced_refs[i].at[n] for n in range(nodes)]
        if i + 1 < count:
            update(targets[i + 1], tier - 1, row_ref, coupling_ref, first, tier * knots)
    for below in range(top - 1, -1, -1):
        update(targets[count + top - 1 - below], below, row_ref, coupling_ref)
    forward(source_refs, coupling_ref, right_ref, own_ref, count, [0])


def whole_call(kernel, args, shapes, scratch, name, limit=8, flops=10**10):
    return pl.pallas_call(
        kernel,
        in_specs=[vmem] * len(args),
        out_specs=[vmem] * len(shapes),
        out_shape=[jax.ShapeDtypeStruct(shape, f32) for shape in shapes],
        scratch_shapes=[pltpu.VMEM(shape, f32) for shape in scratch],
        compiler_params=pltpu.CompilerParams(vmem_limit_bytes=limit * 2**20),
        cost_estimate=pl.CostEstimate(flops=flops, bytes_accessed=2**20, transcendentals=0),
        name=name,
    )(*args)


def leaf_tier(slots, basis_table, turned, prior_precision, top):
    tier_count, _, knots = basis_table.shape
    tier = tier_count - 1
    leaves = len(slots)
    shapes = [(leaves, knots, knots)] + [(leaves, knots, tier * knots)] * 2
    shapes += [(2 ** (t - top), knots, (t + 1) * knots) for t in range(tier - 1, top - 1, -1)]
    shapes.append((top, knots, top * knots))
    inverse, coupling, row, *lower, rest = whole_call(
        functools.partial(leaf_kernel, top=top),
        (basis_table, turned, prior_precision, *slots),
        shapes, [(leaves, knots, knots)], "leaf_tier", limit=16, flops=2 * 10**10,
    )
    return inverse, coupling, row, lower, rest


def inner_tiers(slots, row, inverse, coupling, lower, rest, prior_precision, top):
    knots = prior_precision.shape[1]
    fields = slots[0].shape[0]
    count = len(lower)
    nodes = [value.shape[0] for value in lower]
    shapes = [coupling.shape] + [(n, knots, knots) for n in nodes]
    shapes += [(n, knots, value.shape[2] - knots) for n, value in zip(nodes, lower)]
    shapes += [rest.shape, (1, fields, top * knots), (fields, (count + 1) * knots)]
    scratch = [(max(nodes), knots, knots)] + [value.shape for value in lower]
    scratch += [(n, fields, value.shape[2]) for n, value in zip(nodes, lower)]
    out = whole_call(
        functools.partial(inner_kernel, top=top, count=count, leaves=len(slots)),
        (*slots, row, inverse, coupling, *lower, rest, prior_precision),
        shapes, scratch, "inner_tiers", limit=16, flops=2 * 10**10,
    )
    rest = out[-3].reshape(top * knots, top * knots)
    inverses, couplings = [inverse, *out[1:count + 1]], [out[0], *out[count + 1:-3]]
    return inverses, couplings, rest, out[-2][0], out[-1]


def composites(own_ref, refs, local_ref, deep_ref):
    count = len(refs) // 2
    inverse_refs, coupling_refs = refs[:count], refs[count:]
    knots = inverse_refs[0].shape[1]
    wide = deep_ref.shape[1]

    def solve(depth):
        place = slice((count - 1 - depth) * knots, (count - depth) * knots)
        own = own_ref[:, depth * knots:(depth + 1) * knots]
        local_ref[:, place] = dot_hi(own, inverse_refs[depth][0])

    def shorten(depth):
        first = (count - 1 - depth) * knots
        deep = coupling_refs[depth][0, :, :wide]
        if first > 0:
            between = coupling_refs[depth][0, :, wide:]
            deep = deep - dot_hi(between, deep_ref[:first, :])
            local_ref[:, first:first + knots] -= dot_nt(local_ref[:, :first], between, highest)
        deep_ref[first:first + knots, :] = deep

    depths = range(count - 1, -1, -1)
    return [functools.partial(solve, d) for d in depths] + [
        functools.partial(shorten, d) for d in depths
    ]


def top_step(total, prior_row, inverse_ref, panel_ref, others):
    knots = inverse_ref.shape[0]
    row = total[knots:]
    inverse_ref[...] = row[:, knots:] + diagonal(prior_row)
    invert([inverse_ref], [panel_ref], others)
    coupling = dot_hi(inverse_ref[...], row[:, :knots])
    return coupling, total[:knots, :knots] - dot_tn(row[:, :knots], coupling)


def root_step(schur, prior_row, inverse_ref, panel_ref):
    inverse_ref[...] = schur + diagonal(prior_row)
    invert([inverse_ref], [panel_ref])


def top_kernel(rest_ref, other_ref, prior_ref, own_ref, *refs, both):
    refs, outs = refs[:-6], refs[-6:]
    local_ref, deep_ref, top_ref, coupling_ref, last_ref, panel_ref = outs
    coupling_ref[...], schur = top_step(
        rest_ref[...] + other_ref[...], prior_ref[1:2, :], top_ref, panel_ref,
        composites(own_ref, refs, local_ref, deep_ref),
    )
    if both:
        root_step(schur, prior_ref[0:1, :], last_ref, panel_ref)
    else:
        last_ref[...] = schur


def root_kernel(schur_ref, prior_ref, root_ref, panel_ref):
    root_step(schur_ref[...], prior_ref[0:1, :], root_ref, panel_ref)


def right_kernel(right_ref, other_ref, coupling_ref, out_ref):
    knots = coupling_ref.shape[0]
    right = right_ref[...] + other_ref[...]
    out_ref[:, knots:] = right[:, knots:]
    out_ref[:, :knots] = right[:, :knots] - dot_hi(right[:, knots:], coupling_ref[...])


def descend_kernel(right_ref, other_ref, top_ref, coupling_ref, root_ref, local_ref, deep_ref,
                   out_ref, *, reduced):
    knots = top_ref.shape[0]
    right = right_ref[...]
    if reduced:
        root_right = right[:, :knots]
    else:
        right = right + other_ref[...]
        root_right = right[:, :knots] - dot_hi(right[:, knots:], coupling_ref[...])
    first = dot_hi(root_right, root_ref[...])
    second = dot_hi(right[:, knots:], top_ref[...]) - dot_nt(first, coupling_ref[...], highest)
    tops = jnp.concatenate([first, second], axis=1)
    out_ref[:, :2 * knots] = tops
    out_ref[:, 2 * knots:] = local_ref[...] - dot_nt(tops, deep_ref[...], highest)


def path_weights(rest, right, own, prior_precision, inverses, couplings, leaves):
    knots = prior_precision.shape[1]
    fields = right.shape[0]
    square = (knots, knots)
    region_count = lax.axis_size("region")
    other_right = moved(right, leaves, (leaves // 2, 1), (leaves // 2, 1))
    reduced = region_count > leaves
    args = (rest, swapped(rest, "obs", 1), prior_precision, own, *inverses, *couplings)
    shapes = [(fields, own.shape[1]), (own.shape[1], 2 * knots), square, square, square]
    local, deep, top, coupling, root = whole_call(
        functools.partial(top_kernel, both=not reduced), args, shapes, [square], "top"
    )
    if reduced:
        schur = sum_over(root, "region", leaves, region_count)
        root = whole_call(root_kernel, (schur, prior_precision), [square], [square], "root")[0]
        right = whole_call(right_kernel, (right, other_right, coupling), [right.shape], [], "right")[0]
        other_right = sum_over(right[:, :knots], "region", leaves, region_count)
        right = jnp.concatenate([other_right, right[:, knots:]], axis=1)
    args = (right, other_right, top, coupling, root, local, deep)
    shape = (fields, prior_precision.shape[0] * knots)
    kernel = functools.partial(descend_kernel, reduced=reduced)
    return whole_call(kernel, args, [shape], [], "descend", flops=10**9)[0]


def fitted_kernel(pattern_ref, amplitude_ref, weight_ref, turned_ref, out_ref, table):
    tier_count, knots, pattern_count = turned_ref.shape
    field_count = weight_ref.shape[0]

    @pl.when(pl.program_id(0) == 0)
    def _():
        for tier in range(tier_count):
            high, low = split(weight_ref[:, tier * knots:(tier + 1) * knots])
            table[tier * field_count:(tier + 1) * field_count, :] = (
                dot(high, turned_ref[tier]) + dot(low, turned_ref[tier])
            ).astype(bf16)

    picked = dot(table[...], one_hot(pattern_ref[...], pattern_count))
    amp = amplitude_ref[...]
    total = picked[:field_count] * amp[0:1]
    for tier in range(1, tier_count):
        total = total + picked[tier * field_count:(tier + 1) * field_count] * amp[tier:tier + 1]
    out_ref[...] = total


def fitted_fields(pattern, amplitude, weights, turned):
    tier_count, knots, pattern_count = turned.shape
    obs = pattern.shape[0]
    field_count = weights.shape[0]
    block = min(4096, obs)
    return pl.pallas_call(
        fitted_kernel,
        grid=(obs // block,),
        in_specs=[
            pl.BlockSpec((1, block), lambda i: (0, i)),
            pl.BlockSpec((tier_count, block), lambda i: (0, i)),
            pl.BlockSpec(weights.shape, lambda i: (0, 0)),
            pl.BlockSpec(turned.shape, lambda i: (0, 0, 0)),
        ],
        out_specs=pl.BlockSpec((field_count, block), lambda i: (0, i)),
        out_shape=jax.ShapeDtypeStruct((field_count, obs), f32),
        scratch_shapes=[pltpu.VMEM((tier_count * field_count, pattern_count), bf16)],
        compiler_params=pltpu.CompilerParams(vmem_limit_bytes=16 * 2**20),
        name="fitted_fields",
    )(pattern.reshape(1, obs), amplitude, weights, turned)


def swapped(value, axis, mask):
    pairs = [(source, source ^ mask) for source in range(lax.axis_size(axis))]
    return lax.ppermute(value, axis, pairs)


def sum_over(value, axis, first_mask, size):
    mask = first_mask
    while mask < size:
        value = value + swapped(value, axis, mask)
        mask *= 2
    return value


def in_own_half(leaves):
    return (lax.axis_index("region") % leaves) // (leaves // 2) == lax.axis_index("obs") % 2


def moved(value, leaves, own_move, other_move):
    region_count, obs_count = lax.axis_size("region"), lax.axis_size("obs")
    pairs = []
    for region in range(region_count):
        for obs in range(obs_count):
            own = (region % leaves) // (leaves // 2) == obs % 2
            region_mask, obs_mask = own_move if own else other_move
            target = (region ^ region_mask) * obs_count + (obs ^ obs_mask)
            pairs.append((region * obs_count + obs, target))
    return lax.ppermute(value, ("region", "obs"), pairs)


def sum_for_half(value, leaves):
    half = leaves // 2
    parts = lax.axis_size("obs") // 2
    got = [
        moved(value, leaves, (0, 2 * max(offset, 1)), (half, 1 ^ 2 * offset))
        for offset in range(parts)
    ]
    own = value
    for part in got[1:]:
        own = own + part
    other = got[0]
    for part in got[1:]:
        other = other + part
    return jnp.where(in_own_half(leaves), own, other)


def gather_half(value, leaves):
    return [value] + [swapped(value, "region", offset) for offset in range(1, leaves // 2)]


def spread_weights(weights, leaves):
    return jnp.where(in_own_half(leaves), weights, swapped(weights, "obs", 1))


def shards(pattern, amplitude, basis_table, fields, prior_precision):
    tier_count = basis_table.shape[0]
    leaves = 2 ** (tier_count - 2)
    order = tier_count * basis_table.shape[2]
    turned = jnp.swapaxes(basis_table, 1, 2)
    sums = statistics(pattern, amplitude, fields, basis_table)
    pair_rows = sums.shape[0] - fields.shape[0]
    sums = sums + swapped(sums, "obs", 1)
    pairs, project = sums[:pair_rows, :basis_table.shape[1]], sums[pair_rows:, :order]
    pairs = sum_for_half(pairs, leaves)
    project = sum_over(project, "obs", 2, lax.axis_size("obs"))
    pair_slots = gather_half(pairs, leaves)
    project_slots = gather_half(project, leaves)
    inverse, coupling, row, lower, rest = leaf_tier(
        pair_slots, basis_table, turned, prior_precision, 2
    )
    inverses, couplings, rest, right, own = inner_tiers(
        project_slots, row, inverse, coupling, lower, rest, prior_precision, 2
    )
    weights = path_weights(rest, right, own, prior_precision, inverses, couplings, leaves)
    weights = spread_weights(weights, leaves)
    return fitted_fields(pattern, amplitude, weights, turned)


def solution(mesh):
    return jax.shard_map(
        shards,
        mesh=mesh,
        in_specs=(
            P(("region", "obs")),
            P(None, ("region", "obs")),
            P(),
            P(None, ("region", "obs")),
            P(),
        ),
        out_specs=P(None, ("region", "obs")),
        check_vma=False,
    )
```
